128 devices in a mesh: src: 2 (over core), py: 8 (over x, z_hi), pz: 8 (over y, z_lo).
Axes of the slice: x: 4, y: 4, z: 4 (z_hi: 2, z_lo: 2; z = z_hi * 2 + z_lo), core: 2. Of those that a mesh axis runs over, the one named last changes fastest.
Arguments:
- speed: float32 [256, 256, 256], P('pz', 'py'), may hold values from 0.965 to 1.035
- sign_bits: int32 [2, 1024], P('src'), may hold values from 0 to 1
- positions: int32 [3, 1024], replicated, may hold values from 0 to 255
- observed: float32 [2, 2, 256, 256, 256], P('src', None, 'pz', 'py'), may hold values from -3 to 3
Outputs:
- fields: float32 [2, 2, 256, 256, 256], P('src', None, 'pz', 'py')
- gradient: float32 [256, 256, 256], P('pz', 'py', 'src')
The draws below stay inside these ranges and needn't reach their ends.
All inputs are finite; a program needn't handle non-finite values.
Results may differ from the reference program's by a relative error of at most 0.00022.
Values sent between devices are 32-bit elements; how exact they have to be, the bound alone decides.
A program may use at most 128 MiB of HBM per device.

```python
import math
import jax
import jax.numpy as jnp
from jax import lax

N = 256
EMITTERS = 1024
ITERS = 2
PATTERNS = 2


def plant(array, key, low, largest):
    place = [jax.random.randint(jax.random.fold_in(key, axis), (), 0, length) for axis, length in enumerate(array.shape)]
    main_axis = array.shape.index(max(array.shape))
    neighbour = place[:main_axis] + [(place[main_axis] + 1) % array.shape[main_axis]] + place[main_axis + 1:]
    return array.at[tuple(place)].set(low).at[tuple(neighbour)].set(largest)


def steps_of(stream_key, shape, pieces, low, largest):
    loudness, own = 1.0, jax.random.fold_in(stream_key, 6)
    for position, shards_of in pieces:
        draws = jnp.exp(jax.random.uniform(jax.random.fold_in(own, position), (shards_of,), jnp.float32, low / len(pieces), largest / len(pieces)))
        loudness = loudness * jnp.repeat(draws, shape[position] // shards_of).reshape([-1 if axis == position else 1 for axis in range(len(shape))])
    return loudness


def gaussian(key, extent, width, reach, shards=(), held_as=jnp.bfloat16):
    values = width * jax.random.normal(key, extent, jnp.float32)
    if shards:
        values = values * steps_of(key, extent, shards, -0.22, 0.18)
    return jnp.clip(values, -reach, reach).astype(held_as)


def setup_inputs(seed: int = 0) -> dict:
    keys = jax.random.split(jax.random.key(seed), 5)
    speed = jnp.clip(0.965 + 0.06999999 * jax.random.uniform(keys[0], (N, N, N), jnp.float32) ** steps_of(keys[0], (N, N, N), ((0, 8), (1, 8)), -0.2, 0.2), 0.965, 1.035)
    sign_bits = plant(jax.random.randint(keys[1], (PATTERNS, EMITTERS), 0, 2), jax.random.fold_in(keys[1], 1), 0, 1).astype(jnp.int32)
    positions = plant(jax.random.randint(keys[2], (3, EMITTERS), 0, N), jax.random.fold_in(keys[2], 1), 0, N - 1).astype(jnp.int32)
    observed = gaussian(keys[3], (PATTERNS, 2, N, N, N), 0.5, 3.0, ((0, 2), (2, 8), (3, 8)), jnp.float32)
    return {"speed": speed, "sign_bits": sign_bits, "positions": positions, "observed": observed}


wave_sq = (2.0 * math.pi / 8.0) ** 2
damping = 0.05
source_gain = 40.0


def wavenumber(length, start, count):
    freq = start + jnp.arange(count, dtype=jnp.int32)
    signed = jnp.where(freq < length // 2, freq, freq - length)
    return signed.astype(jnp.float32) * (2.0 * math.pi / length)


def green(first, second, third):
    shifted = first[:, None, None] ** 2 + second[None, :, None] ** 2 + third[None, None, :] ** 2 - wave_sq
    denom = shifted * shifted + damping * damping
    return shifted / denom, damping / denom


def reference(speed, sign_bits, positions, observed):
    length = speed.shape[0]
    flat = (positions[0] * length + positions[1]) * length + positions[2]
    weights_all = (2 * sign_bits - 1).astype(jnp.float32) * source_gain
    inverse_sq = 1.0 / (speed * speed)
    real_v = wave_sq * (inverse_sq - 1.0)
    ratio = real_v / damping
    unity = jnp.ones_like(real_v)
    potential = lax.complex(real_v, -damping * unity)
    precond = lax.complex(unity, ratio)
    waves = wavenumber(length, 0, length)
    green_re, green_im = green(waves, waves, waves)
    symbol = lax.complex(green_re, green_im)

    def solve(items):
        weights, seen = items
        source = jnp.zeros((length * length * length,), jnp.float32).at[flat].add(weights)
        source = source.reshape(length, length, length)
        zeros_field = jnp.zeros((length, length, length), speed.dtype)
        field = lax.complex(zeros_field, zeros_field)
        for step in range(ITERS):
            drive = potential * field + source
            spread = jnp.fft.ifftn(symbol * jnp.fft.fftn(drive))
            field = field + precond * (spread - field)
        real_part = jnp.real(field)
        imag_part = jnp.imag(field)
        term = (real_part - seen[0]) * real_part + (imag_part - seen[1]) * imag_part
        return jnp.stack([real_part, imag_part]), term

    fields, terms = lax.map(solve, (weights_all, observed))
    gradient = jnp.sum(terms, axis=0) * (-2.0 * wave_sq) * inverse_sq / speed
    return fields, gradient
```

```python
import functools
import math

import jax
import jax.numpy as jnp
import numpy as np
from jax import lax
from jax.experimental import pallas as pl
from jax.experimental.pallas import tpu as pltpu
from jax.sharding import PartitionSpec as P

MESH = pl.DeviceIdType.MESH
N = 256
SIDE = 8
CHIPS = SIDE * SIDE
BLOCK = N // SIDE
ROWS = BLOCK * BLOCK
LANES = 128
HALVES = 2
PIECES = 1
TILES = 4 // PIECES
MSG = TILES * 8
ORDER = 27

wave_sq = (2.0 * math.pi / 8.0) ** 2
damping = 0.05
source_gain = 40.0


def tables():
    angle = lambda a, b: 2.0 * np.pi * ((a[:, None] * b[None, :]) % N) / N
    count = np.arange(N)
    chip = np.arange(CHIPS)
    freq = np.stack([2 * chip, (N - 2 * chip) % N, 2 * chip + 1, N - 1 - 2 * chip], 1)
    freq[0, 1] = N // 2
    rows = []
    for half in range(HALVES):
        for member in range(2):
            turn = angle(freq[:, 2 * half + member], count)
            rows.append(np.concatenate([np.cos(turn), np.sin(turn)], 1))
            rows.append(np.concatenate([-np.sin(turn), np.cos(turn)], 1))
    along_x = np.concatenate(rows, 0)
    turn = angle(count, count)
    cosine, sine = np.cos(turn), np.sin(turn)
    along_y = np.block([[cosine, -sine], [sine, cosine]])
    order = z_of_row(count)
    forward = np.concatenate([cosine[:, order], sine[:, order]], 0)
    backward = np.concatenate([cosine[order], sine[order]], 0)
    out = []
    for table in (along_x, along_y, forward, backward):
        high = table.astype(jnp.bfloat16)
        out += [high, (table - high.astype(np.float64)).astype(jnp.bfloat16)]
    return out


def z_of_row(row):
    per = N // PIECES
    piece, rest = row // per, row % per
    s, rest = rest // (16 * TILES), rest % (16 * TILES)
    j, rest = rest // (2 * TILES), rest % (2 * TILES)
    return j * BLOCK + 8 * (piece * TILES) + 4 * rest + s


def split(value):
    high = value.astype(jnp.bfloat16)
    return high, (value - high.astype(jnp.float32)).astype(jnp.bfloat16)


def times(value, high, low):
    first, rest = split(value)
    dot = functools.partial(jnp.dot, preferred_element_type=jnp.float32)
    return dot(first, high) + (dot(first, low) + dot(rest, high))


def times_left(high, low, value):
    first, rest = split(value)
    dot = functools.partial(jnp.dot, preferred_element_type=jnp.float32)
    return dot(high, first) + (dot(low, first) + dot(high, rest))


def swap(parts):
    lane = lax.broadcasted_iota(jnp.int32, parts[0].shape, 1)
    odd, upper = (lane & 32) != 0, (lane & 64) != 0
    mid = []
    for b in (0, 2):
        low, high = parts[b], parts[b + 1]
        mid.append(jnp.where(odd, pltpu.roll(high, 32, 1), low))
        mid.append(jnp.where(odd, high, pltpu.roll(low, 96, 1)))
    out = [None] * 4
    for b in (0, 1):
        low, high = mid[b], mid[b + 2]
        out[b] = jnp.where(upper, pltpu.roll(high, 64, 1), low)
        out[b + 2] = jnp.where(upper, high, pltpu.roll(low, 64, 1))
    return out


def kernel(
    speed_hbm, bits_ref, pos_ref, seen_hbm, xh, xl, yh, yl, fh, fl, bh, bl,
    field_hbm, grad_ref,
    sent, got, acc, first, green, plane, drive_h, drive_l, source, speed, seen, field, term, other,
    send_sem, recv_sem, copy_sem, pair_send, pair_recv,
):
    core, py, pz = lax.axis_index("src"), lax.axis_index("py"), lax.axis_index("pz")
    me = py * SIDE + pz
    X, ZH, Y, ZL = py // 2, py % 2, pz // 2, pz % 2
    Z = 2 * ZH + ZL

    def partner(k):
        o = (k * ORDER) % CHIPS
        x, y, z = (X + o // 16) % 4, (Y + o // 4) % 4, (Z + o) % 4
        return 2 * x + z // 2, 2 * y + z % 2

    barrier = pltpu.get_barrier_semaphore()

    @pl.loop(1, CHIPS)
    def _(k):
        a, b = partner(k)
        pl.semaphore_signal(barrier, inc=1, device_id={"py": a, "pz": b}, device_id_type=MESH)

    pl.semaphore_signal(barrier, inc=1, device_id={"src": 1 - core}, device_id_type=MESH)

    get_speed = pltpu.make_async_copy(speed_hbm, speed, copy_sem.at[0])
    get_seen = pltpu.make_async_copy(seen_hbm, seen, copy_sem.at[1])
    get_speed.start()
    get_seen.start()

    def slot(phase, half, piece):
        return (phase * HALVES + half) * PIECES + piece

    def send(phase, half, piece):
        n = slot(phase, half, piece)
        mine = pl.ds(pl.multiple_of(me * MSG, MSG), MSG)

        @pl.loop(1, CHIPS)
        def _(k):
            a, b = partner(k)
            theirs = pl.ds(pl.multiple_of((a * SIDE + b) * MSG, MSG), MSG)
            pltpu.make_async_remote_copy(
                src_ref=sent.at[n, theirs],
                dst_ref=got.at[n, mine],
                send_sem=send_sem.at[n],
                recv_sem=recv_sem.at[n],
                device_id={"py": a, "pz": b},
                device_id_type=MESH,
            ).start()

        got[n, mine] = sent[n, mine]

    def finish(n, sem):
        everyone = got.at[n, pl.ds(0, (CHIPS - 1) * MSG)]
        pltpu.make_async_copy(everyone, everyone, sem.at[n]).wait()

    def arrive(phase, half, piece):
        finish(slot(phase, half, piece), recv_sem)

    def wave_of(index):
        signed = jnp.where(index < N // 2, index, index - N)
        return signed.astype(jnp.float32) * (2.0 * math.pi / N)

    row_id = lax.broadcasted_iota(jnp.int32, (N, N), 0)
    lane_id = lax.broadcasted_iota(jnp.int32, (N, N), 1)
    base = wave_of(row_id) ** 2 + wave_of(lane_id) ** 2

    def green_of(half, member):
        index = 2 * me + half
        if half == 0 and member == 1:
            index = jnp.where(me == 0, N // 2, index)
        wave = index.astype(jnp.float32) * (2.0 * math.pi / N)
        shifted = base + wave * wave - wave_sq
        scale = (1.0 / N**3) / (shifted * shifted + damping * damping)
        green[2 * half + member, :, 0:N] = shifted * scale
        green[2 * half + member, :, N : 2 * N] = damping * scale

    def spectrum_z(value):
        both = times_left(fh[...], fl[...], value)
        real = both[:N, :N] + both[N:, N:]
        imag = both[:N, N:] - both[N:, :N]
        return real, imag

    def filtered(half, member, real, imag):
        g_re = green[2 * half + member, :, 0:N]
        g_im = green[2 * half + member, :, N : 2 * N]
        plane[member * N : (member + 1) * N, 0:N] = real * g_im + imag * g_re
        plane[member * N : (member + 1) * N, N : 2 * N] = real * g_re - imag * g_im

    def inverse(phase, half):
        plane[...] = times(plane[...], yh[...], yl[...])
        for member in range(2):
            both = times_left(bh[...], bl[...], plane[member * N : (member + 1) * N, :])
            real = both[:N, N:] - both[N:, :N]
            imag = both[:N, :N] + both[N:, N:]
            size = 16 * TILES
            for part, value in ((0, real), (1, imag)):
                for piece in range(PIECES):
                    n = slot(phase, half, piece)
                    for h in range(2):
                        rows = [
                            value[(piece * 4 + s) * size : (piece * 4 + s + 1) * size, h * LANES : (h + 1) * LANES]
                            for s in range(4)
                        ]
                        for b, block in enumerate(swap(rows)):
                            start = (4 * h + b) * SIDE * MSG + 2 * member + part
                            sent[n, pl.ds(start, size, stride=4), :] = block

    def gather(phase, half):
        size = 16 * TILES
        for piece in range(PIECES):
            n = slot(phase, half, piece)
            for member in range(2):
                for part in range(2):
                    for h in range(2):
                        rows = [
                            got[n, pl.ds((4 * h + b) * SIDE * MSG + 2 * member + part, size, stride=4), :]
                            for b in range(4)
                        ]
                        for s, block in enumerate(swap(rows)):
                            at = member * N + (piece * 4 + s) * size
                            plane[at : at + size, part * N + h * LANES : part * N + (h + 1) * LANES] = block

    weight = (2 * bits_ref[...] - 1).astype(jnp.float32) * source_gain
    emitters = weight.shape[1]
    z_at, y_at, x_at = pos_ref[0:1, :], pos_ref[1:2, :], pos_ref[2:3, :]
    ids = lax.broadcasted_iota(jnp.int32, (N, emitters), 0)

    def hits(where, index):
        return jnp.where(where == index, 1.0, 0.0).astype(jnp.bfloat16)

    which = lax.broadcasted_iota(jnp.int32, (8, N), 0)
    turn = lax.broadcasted_iota(jnp.int32, (8, N), 1)
    only = jnp.logical_and(which == 1, me == 0)
    turn = (turn * jnp.where(only, N // 2, 2 * me + which // 2)) & (N - 1)
    shift = jnp.where(jnp.logical_and(which % 2 == 1, jnp.logical_not(only)), math.pi / 2.0, 0.0)
    wave_rows = jnp.cos(turn.astype(jnp.float32) * (2.0 * math.pi / N) - shift)
    wh, wl = split(wave_rows)
    x_hits = hits(x_at, ids)
    phases = jnp.dot(wh, x_hits, preferred_element_type=jnp.float32) + jnp.dot(
        wl, x_hits, preferred_element_type=jnp.float32
    )
    phases = phases * weight
    y_hits = hits(y_at, ids)
    z_equal = z_at == z_of_row(ids)

    nt = (((1,), (1,)), ((), ()))
    for half in range(HALVES):
        for member in range(2):
            row = phases[2 * half + member : 2 * half + member + 1, :]
            high = row.astype(jnp.bfloat16).astype(jnp.float32)
            value = 0.0
            for piece_row in (high, row - high):
                left = jnp.where(z_equal, piece_row, 0.0).astype(jnp.bfloat16)
                value = value + lax.dot_general(left, y_hits, nt, preferred_element_type=jnp.float32)
            plane[member * N : (member + 1) * N, 0:N] = value
        lines = times(plane[:, 0:N], yh[0:N, :], yl[0:N, :])
        one_re, one_im = spectrum_z(lines[:N])
        two_re, two_im = spectrum_z(lines[N:])
        for member in range(2):
            green_of(half, member)
        plus_re, plus_im = one_re + two_im, one_im - two_re
        minus_re, minus_im = one_re - two_im, one_im + two_re
        if half == 0:
            alone = me == 0
            plus_re, plus_im = jnp.where(alone, one_re, plus_re), jnp.where(alone, one_im, plus_im)
            minus_re, minus_im = jnp.where(alone, two_re, minus_re), jnp.where(alone, two_im, minus_im)
        filtered(half, 0, plus_re, plus_im)
        filtered(half, 1, minus_re, minus_im)
        inverse(0, half)
        if half == 0:
            pl.semaphore_wait(barrier, CHIPS)
        for piece in range(PIECES):
            send(0, half, piece)

    local_z, local_y = z_at - pz * BLOCK, y_at - py * BLOCK
    inside = (local_z >= 0) & (local_z < BLOCK) & (local_y >= 0) & (local_y < BLOCK)
    cell = jnp.where(inside, local_z * BLOCK + local_y, -1)
    lines = jnp.where(x_at == ids, weight, 0.0).astype(jnp.bfloat16)

    @pl.loop(0, ROWS // N)
    def _(g):
        at = pl.multiple_of(g * N, N)
        source[pl.ds(at, N), :] = lax.dot_general(
            hits(cell - at, ids), lines, nt, preferred_element_type=jnp.float32
        )

    get_speed.wait()

    def x_inverse(phase, half, piece, tile, r):
        n = slot(phase, half, piece)
        rows = [got[n, pl.ds(tile * 8 + r * 4 + kc, CHIPS, stride=MSG), :] for kc in range(4)]
        return times(jnp.concatenate(rows, 0).T, xh[half * N : (half + 1) * N, :], xl[half * N : (half + 1) * N, :])

    def x_forward(phase, half, piece, tile):
        n = slot(phase, half, piece)
        at = pl.multiple_of((piece * TILES + tile) * N, N)
        high, low = drive_h[pl.ds(at, N), :], drive_l[pl.ds(at, N), :]
        table_h, table_l = xh[half * N : (half + 1) * N, :], xl[half * N : (half + 1) * N, :]
        dot = lambda a, b: lax.dot_general(a, b, nt, preferred_element_type=jnp.float32)
        out = dot(table_h, high) + (dot(table_l, high) + dot(table_h, low))
        for r in range(2):
            for kc in range(4):
                sent[n, pl.ds(tile * 8 + r * 4 + kc, CHIPS, stride=MSG), :] = out[
                    kc * CHIPS : (kc + 1) * CHIPS, r * LANES : (r + 1) * LANES
                ]

    def half_inverse(phase):
        for piece in range(PIECES):
            arrive(phase, 0, piece)

            @pl.loop(0, TILES)
            def _(tile):
                for r in range(2):
                    at = pl.multiple_of((piece * TILES + tile) * N + r * LANES, LANES)
                    acc[pl.ds(at, LANES), :] = x_inverse(phase, 0, piece, tile, r)

    def medium(at):
        v = speed[pl.ds(at, LANES), :]
        inverse_sq = 1.0 / (v * v)
        real_v = wave_sq * (inverse_sq - 1.0)
        return v, inverse_sq, real_v

    half_inverse(0)
    for piece in range(PIECES):
        arrive(0, 1, piece)

        @pl.loop(0, TILES)
        def _(tile):
            for r in range(2):
                at = pl.multiple_of((piece * TILES + tile) * N + r * LANES, LANES)
                here = pl.ds(at, LANES)
                spread = acc[here, :] + x_inverse(0, 1, piece, tile, r)
                spread_re, spread_im = spread[:, :N], spread[:, N:]
                _, _, real_v = medium(at)
                ratio = real_v / damping
                real, imag = spread_re - ratio * spread_im, spread_im + ratio * spread_re
                first[here, 0:N] = real
                first[here, N : 2 * N] = imag
                drive_re = real_v * real + damping * imag + source[here, :]
                drive_im = real_v * imag - damping * real
                for part, value in ((0, drive_re), (1, drive_im)):
                    high, low = split(value)
                    drive_h[here, part * N : (part + 1) * N] = high
                    drive_l[here, part * N : (part + 1) * N] = low
            x_forward(1, 0, piece, tile)

        send(1, 0, piece)
    for piece in range(PIECES):

        @pl.loop(0, TILES)
        def _(tile):
            x_forward(1, 1, piece, tile)

        send(1, 1, piece)

    for half in range(HALVES):
        for piece in range(PIECES):
            arrive(1, half, piece)
        gather(1, half)
        plane[...] = times(plane[...], yh[...], yl[...])
        for member in range(2):
            real, imag = spectrum_z(plane[member * N : (member + 1) * N, :])
            filtered(half, member, real, imag)
        inverse(2, half)
        for piece in range(PIECES):
            send(2, half, piece)

    half_inverse(2)
    get_seen.wait()
    for piece in range(PIECES):
        arrive(2, 1, piece)

        @pl.loop(0, TILES)
        def _(tile):
            for r in range(2):
                at = pl.multiple_of((piece * TILES + tile) * N + r * LANES, LANES)
                here = pl.ds(at, LANES)
                spread = acc[here, :] + x_inverse(2, 1, piece, tile, r)
                was_re, was_im = first[here, 0:N], first[here, N : 2 * N]
                delta_re, delta_im = spread[:, :N] - was_re, spread[:, N:] - was_im
                v, inverse_sq, real_v = medium(at)
                ratio = real_v / damping
                real = was_re + delta_re - ratio * delta_im
                imag = was_im + delta_im + ratio * delta_re
                field[0, here, :] = real
                field[1, here, :] = imag
                misfit = (real - seen[0, here, :]) * real + (imag - seen[1, here, :]) * imag
                part = misfit * (-2.0 * wave_sq) * inverse_sq / v
                term[0, here, :] = part[:, :LANES]
                term[1, here, :] = part[:, LANES:]

    swap_terms = pltpu.make_async_remote_copy(
        src_ref=term.at[1 - core],
        dst_ref=other,
        send_sem=pair_send,
        recv_sem=pair_recv,
        device_id={"src": 1 - core},
        device_id_type=MESH,
    )
    swap_terms.start()
    put_field = pltpu.make_async_copy(field, field_hbm, copy_sem.at[0])
    put_field.start()
    swap_terms.wait()
    grad_ref[...] = term[core] + other[...]
    for n in range(3 * HALVES * PIECES):
        finish(n, send_sem)
    put_field.wait()


def per_device(speed, sign_bits, positions, observed):
    f32, bf16 = jnp.float32, jnp.bfloat16
    anywhere = pl.BlockSpec(memory_space=pl.ANY)
    vmem = pl.BlockSpec(memory_space=pltpu.VMEM)
    slots = 3 * HALVES * PIECES
    field, gradient = pl.pallas_call(
        kernel,
        out_shape=(
            jax.ShapeDtypeStruct((2, ROWS, N), f32),
            jax.ShapeDtypeStruct((ROWS, LANES), f32),
        ),
        in_specs=[anywhere, vmem, vmem, anywhere] + [vmem] * 8,
        out_specs=(anywhere, vmem),
        scratch_shapes=[
            pltpu.VMEM((slots, CHIPS * MSG, LANES), f32),
            pltpu.VMEM((slots, CHIPS * MSG, LANES), f32),
            pltpu.VMEM((ROWS, 2 * N), f32),
            pltpu.VMEM((ROWS, 2 * N), f32),
            pltpu.VMEM((4, N, 2 * N), f32),
            pltpu.VMEM((2 * N, 2 * N), f32),
            pltpu.VMEM((ROWS, 2 * N), bf16),
            pltpu.VMEM((ROWS, 2 * N), bf16),
            pltpu.VMEM((ROWS, N), f32),
            pltpu.VMEM((ROWS, N), f32),
            pltpu.VMEM((2, ROWS, N), f32),
            pltpu.VMEM((2, ROWS, N), f32),
            pltpu.VMEM((2, ROWS, LANES), f32),
            pltpu.VMEM((ROWS, LANES), f32),
            pltpu.SemaphoreType.DMA((slots,)),
            pltpu.SemaphoreType.DMA((slots,)),
            pltpu.SemaphoreType.DMA((2,)),
            pltpu.SemaphoreType.DMA,
            pltpu.SemaphoreType.DMA,
        ],
        compiler_params=pltpu.CompilerParams(
            collective_id=0, has_side_effects=True, vmem_limit_bytes=60 << 20
        ),
    )(
        speed.reshape(ROWS, N),
        sign_bits,
        positions,
        observed.reshape(2, ROWS, N),
        *[jnp.asarray(t) for t in tables()],
    )
    return field.reshape(1, 2, BLOCK, BLOCK, N), gradient.reshape(BLOCK, BLOCK, LANES)


def solution(mesh):
    return jax.shard_map(
        per_device,
        mesh=mesh,
        in_specs=(P("pz", "py", None), P("src", None), P(), P("src", None, "pz", "py", None)),
        out_specs=(P("src", None, "pz", "py", None), P("pz", "py", "src")),
        check_vma=False,
    )
```

```python
import functools
import math

import jax
import jax.numpy as jnp
import numpy as np
from jax import lax
from jax.experimental import pallas as pl
from jax.experimental.pallas import tpu as pltpu
from jax.sharding import PartitionSpec as P

MESH = pl.DeviceIdType.MESH
N = 256
SIDE = 8
CHIPS = SIDE * SIDE
BLOCK = N // SIDE
ROWS = BLOCK * BLOCK
LANES = 128
HALVES = 2
PIECES = 2
TILES = 4 // PIECES
MSG = TILES * 8
ORDER = 27

wave_sq = (2.0 * math.pi / 8.0) ** 2
damping = 0.05
source_gain = 40.0


def tables():
    angle = lambda a, b: 2.0 * np.pi * ((a[:, None] * b[None, :]) % N) / N
    count = np.arange(N)
    chip = np.arange(CHIPS)
    freq = np.stack([2 * chip, (N - 2 * chip) % N, 2 * chip + 1, N - 1 - 2 * chip], 1)
    freq[0, 1] = N // 2
    rows = []
    for half in range(HALVES):
        for member in range(2):
            turn = angle(freq[:, 2 * half + member], count)
            rows.append(np.concatenate([np.cos(turn), np.sin(turn)], 1))
            rows.append(np.concatenate([-np.sin(turn), np.cos(turn)], 1))
    along_x = np.concatenate(rows, 0)
    turn = angle(count, count)
    cosine, sine = np.cos(turn), np.sin(turn)
    along_y = np.block([[cosine, -sine], [sine, cosine]])
    order = z_of_row(count)
    forward = np.concatenate([cosine[:, order], sine[:, order]], 0)
    backward = np.concatenate([cosine[order], sine[order]], 0)
    out = []
    for table in (along_y, forward, backward, along_x):
        high = table.astype(jnp.bfloat16)
        out += [high, (table - high.astype(np.float64)).astype(jnp.bfloat16)]
    return out


def z_of_row(row):
    per = N // PIECES
    piece, rest = row // per, row % per
    s, rest = rest // (16 * TILES), rest % (16 * TILES)
    j, rest = rest // (2 * TILES), rest % (2 * TILES)
    return j * BLOCK + 8 * (piece * TILES) + 4 * rest + s


def split(value):
    high = value.astype(jnp.bfloat16)
    return high, (value - high.astype(jnp.float32)).astype(jnp.bfloat16)


def times(value, high, low):
    first, rest = split(value)
    dot = functools.partial(jnp.dot, preferred_element_type=jnp.float32)
    return dot(first, high) + (dot(first, low) + dot(rest, high))


def times_left(high, low, value):
    first, rest = split(value)
    dot = functools.partial(jnp.dot, preferred_element_type=jnp.float32)
    return dot(high, first) + (dot(low, first) + dot(high, rest))


def swap(parts):
    lane = lax.broadcasted_iota(jnp.int32, parts[0].shape, 1)
    odd, upper = (lane & 32) != 0, (lane & 64) != 0
    mid = []
    for b in (0, 2):
        low, high = parts[b], parts[b + 1]
        mid.append(jnp.where(odd, pltpu.roll(high, 32, 1), low))
        mid.append(jnp.where(odd, high, pltpu.roll(low, 96, 1)))
    out = [None] * 4
    for b in (0, 1):
        low, high = mid[b], mid[b + 2]
        out[b] = jnp.where(upper, pltpu.roll(high, 64, 1), low)
        out[b + 2] = jnp.where(upper, high, pltpu.roll(low, 64, 1))
    return out


def kernel(
    speed_hbm, bits_hbm, pos_hbm, seen_hbm, yh_hbm, yl_hbm, fh_hbm, fl_hbm, bh_hbm, bl_hbm, xh_hbm, xl_hbm,
    field, term, other,
    bits_ref, pos_ref, yh, yl, fh, fl, bh, bl, xh, xl, sent, got, acc, first, green, plane, drive_h, drive_l, source, speed, seen,
    send_sem, recv_sem, load_sem, pair_send, pair_recv,
):
    core, py, pz = lax.axis_index("src"), lax.axis_index("py"), lax.axis_index("pz")
    me = py * SIDE + pz
    X, ZH, Y, ZL = py >> 1, py & 1, pz >> 1, pz & 1
    Z = 2 * ZH + ZL

    def partner(k):
        o = (k * ORDER) & (CHIPS - 1)
        x, y, z = (X + (o >> 4)) & 3, (Y + (o >> 2)) & 3, (Z + o) & 3
        return 2 * x + (z >> 1), 2 * y + (z & 1)

    barrier = pltpu.get_barrier_semaphore()

    @pl.loop(1, CHIPS)
    def _(k):
        a, b = partner(k)
        pl.semaphore_signal(barrier, inc=1, device_id={"py": a, "pz": b}, device_id_type=MESH)

    pl.semaphore_signal(barrier, inc=1, device_id={"src": 1 - core}, device_id_type=MESH)

    pairs = ((bits_hbm, bits_ref), (pos_hbm, pos_ref), (yh_hbm, yh), (yl_hbm, yl), (fh_hbm, fh), (fl_hbm, fl), (bh_hbm, bh), (bl_hbm, bl),
             (xh_hbm, xh), (xl_hbm, xl), (speed_hbm, speed), (seen_hbm, seen))
    loads = [pltpu.make_async_copy(a, b, load_sem.at[n]) for n, (a, b) in enumerate(pairs)]
    for load in loads:
        load.start()

    def slot(phase, half, piece):
        return (phase * HALVES + half) * PIECES + piece

    def send(phase, half, piece):
        n = slot(phase, half, piece)
        mine = pl.ds(pl.multiple_of(me * MSG, MSG), MSG)

        @pl.loop(1, CHIPS)
        def _(k):
            a, b = partner(k)
            theirs = pl.ds(pl.multiple_of((a * SIDE + b) * MSG, MSG), MSG)
            pltpu.make_async_remote_copy(
                src_ref=sent.at[n, theirs],
                dst_ref=got.at[n, mine],
                send_sem=send_sem.at[n],
                recv_sem=recv_sem.at[n],
                device_id={"py": a, "pz": b},
                device_id_type=MESH,
            ).start()

        got[n, mine] = sent[n, mine]

    def finish(n, sem):
        everyone = got.at[n, pl.ds(0, (CHIPS - 1) * MSG)]
        pltpu.make_async_copy(everyone, everyone, sem.at[n]).wait()

    def arrive(phase, half, piece):
        finish(slot(phase, half, piece), recv_sem)

    def wave_of(index):
        signed = jnp.where(index < N // 2, index, index - N)
        return signed.astype(jnp.float32) * (2.0 * math.pi / N)

    row_id = lax.broadcasted_iota(jnp.int32, (N, N), 0)
    lane_id = lax.broadcasted_iota(jnp.int32, (N, N), 1)
    base = wave_of(row_id) ** 2 + wave_of(lane_id) ** 2

    def green_of(half, member):
        index = 2 * me + half
        if half == 0 and member == 1:
            index = jnp.where(me == 0, N // 2, index)
        wave = index.astype(jnp.float32) * (2.0 * math.pi / N)
        shifted = base + wave * wave - wave_sq
        scale = (1.0 / N**3) / (shifted * shifted + damping * damping)
        green[2 * half + member, :, 0:N] = shifted * scale
        green[2 * half + member, :, N : 2 * N] = damping * scale

    def spectrum_z(value):
        both = times_left(fh[...], fl[...], value)
        real = both[:N, :N] + both[N:, N:]
        imag = both[:N, N:] - both[N:, :N]
        return real, imag

    def filtered(half, member, real, imag):
        g_re = green[2 * half + member, :, 0:N]
        g_im = green[2 * half + member, :, N : 2 * N]
        plane[member * N : (member + 1) * N, 0:N] = real * g_im + imag * g_re
        plane[member * N : (member + 1) * N, N : 2 * N] = real * g_re - imag * g_im

    def inverse(phase, half):
        plane[...] = times(plane[...], yh[...], yl[...])
        for member in range(2):
            both = times_left(bh[...], bl[...], plane[member * N : (member + 1) * N, :])
            real = both[:N, N:] - both[N:, :N]
            imag = both[:N, :N] + both[N:, N:]
            size = 16 * TILES
            for part, value in ((0, real), (1, imag)):
                for piece in range(PIECES):
                    n = slot(phase, half, piece)
                    for h in range(2):
                        rows = [
                            value[(piece * 4 + s) * size : (piece * 4 + s + 1) * size, h * LANES : (h + 1) * LANES]
                            for s in range(4)
                        ]
                        for b, block in enumerate(swap(rows)):
                            start = (4 * h + b) * SIDE * MSG + 2 * member + part
                            sent[n, pl.ds(start, size, stride=4), :] = block

    def gather(phase, half):
        size = 16 * TILES
        for piece in range(PIECES):
            n = slot(phase, half, piece)
            for member in range(2):
                for part in range(2):
                    for h in range(2):
                        rows = [
                            got[n, pl.ds((4 * h + b) * SIDE * MSG + 2 * member + part, size, stride=4), :]
                            for b in range(4)
                        ]
                        for s, block in enumerate(swap(rows)):
                            at = member * N + (piece * 4 + s) * size
                            plane[at : at + size, part * N + h * LANES : part * N + (h + 1) * LANES] = block

    for load in loads[:2]:
        load.wait()
    weight = (2 * bits_ref[...] - 1).astype(jnp.float32) * source_gain
    emitters = weight.shape[1]
    z_at, y_at, x_at = pos_ref[0:1, :], pos_ref[1:2, :], pos_ref[2:3, :]
    ids = lax.broadcasted_iota(jnp.int32, (N, emitters), 0)

    def hits(where, index):
        return jnp.where(where == index, 1.0, 0.0).astype(jnp.bfloat16)

    which = lax.broadcasted_iota(jnp.int32, (8, N), 0)
    turn = lax.broadcasted_iota(jnp.int32, (8, N), 1)
    only = jnp.logical_and(which == 1, me == 0)
    turn = (turn * jnp.where(only, N // 2, 2 * me + which // 2)) & (N - 1)
    shift = jnp.where(jnp.logical_and(which % 2 == 1, jnp.logical_not(only)), math.pi / 2.0, 0.0)
    wave_rows = jnp.cos(turn.astype(jnp.float32) * (2.0 * math.pi / N) - shift)
    wh, wl = split(wave_rows)
    x_hits = hits(x_at, ids)
    phases = jnp.dot(wh, x_hits, preferred_element_type=jnp.float32) + jnp.dot(
        wl, x_hits, preferred_element_type=jnp.float32
    )
    phases = phases * weight
    y_hits = hits(y_at, ids)
    z_equal = z_at == z_of_row(ids)

    nt = (((1,), (1,)), ((), ()))
    for half in range(HALVES):
        for member in range(2):
            row = phases[2 * half + member : 2 * half + member + 1, :]
            high = row.astype(jnp.bfloat16).astype(jnp.float32)
            value = 0.0
            for piece_row in (high, row - high):
                left = jnp.where(z_equal, piece_row, 0.0).astype(jnp.bfloat16)
                value = value + lax.dot_general(left, y_hits, nt, preferred_element_type=jnp.float32)
            plane[member * N : (member + 1) * N, 0:N] = value
        if half == 0:
            for load in loads[2:8]:
                load.wait()
        lines = times(plane[:, 0:N], yh[0:N, :], yl[0:N, :])
        one_re, one_im = spectrum_z(lines[:N])
        two_re, two_im = spectrum_z(lines[N:])
        for member in range(2):
            green_of(half, member)
        plus_re, plus_im = one_re + two_im, one_im - two_re
        minus_re, minus_im = one_re - two_im, one_im + two_re
        if half == 0:
            alone = me == 0
            plus_re, plus_im = jnp.where(alone, one_re, plus_re), jnp.where(alone, one_im, plus_im)
            minus_re, minus_im = jnp.where(alone, two_re, minus_re), jnp.where(alone, two_im, minus_im)
        filtered(half, 0, plus_re, plus_im)
        filtered(half, 1, minus_re, minus_im)
        inverse(0, half)
        if half == 0:
            pl.semaphore_wait(barrier, CHIPS)
        for piece in range(PIECES):
            send(0, half, piece)

    local_z, local_y = z_at - pz * BLOCK, y_at - py * BLOCK
    inside = (local_z >= 0) & (local_z < BLOCK) & (local_y >= 0) & (local_y < BLOCK)
    cell = jnp.where(inside, local_z * BLOCK + local_y, -1)
    lines = jnp.where(x_at == ids, weight, 0.0).astype(jnp.bfloat16)

    @pl.loop(0, ROWS // N)
    def _(g):
        at = pl.multiple_of(g * N, N)
        source[pl.ds(at, N), :] = lax.dot_general(
            hits(cell - at, ids), lines, nt, preferred_element_type=jnp.float32
        )

    for load in loads[8:11]:
        load.wait()

    def x_inverse(phase, half, piece, tile, r):
        n = slot(phase, half, piece)
        rows = [got[n, pl.ds(tile * 8 + r * 4 + kc, CHIPS, stride=MSG), :] for kc in range(4)]
        return times(jnp.concatenate(rows, 0).T, xh[half * N : (half + 1) * N, :], xl[half * N : (half + 1) * N, :])

    def x_forward(phase, half, piece, tile):
        n = slot(phase, half, piece)
        at = pl.multiple_of((piece * TILES + tile) * N, N)
        high, low = drive_h[pl.ds(at, N), :], drive_l[pl.ds(at, N), :]
        table_h, table_l = xh[half * N : (half + 1) * N, :], xl[half * N : (half + 1) * N, :]
        dot = lambda a, b: lax.dot_general(a, b, nt, preferred_element_type=jnp.float32)
        out = dot(table_h, high) + (dot(table_l, high) + dot(table_h, low))
        for r in range(2):
            for kc in range(4):
                sent[n, pl.ds(tile * 8 + r * 4 + kc, CHIPS, stride=MSG), :] = out[
                    kc * CHIPS : (kc + 1) * CHIPS, r * LANES : (r + 1) * LANES
                ]

    def half_inverse(phase):
        for piece in range(PIECES):
            arrive(phase, 0, piece)

            @pl.loop(0, TILES)
            def _(tile):
                for r in range(2):
                    at = pl.multiple_of((piece * TILES + tile) * N + r * LANES, LANES)
                    acc[pl.ds(at, LANES), :] = x_inverse(phase, 0, piece, tile, r)

    def medium(at):
        v = speed[pl.ds(at, LANES), :]
        inverse_sq = 1.0 / (v * v)
        real_v = wave_sq * (inverse_sq - 1.0)
        return v, inverse_sq, real_v

    half_inverse(0)
    for piece in range(PIECES):
        arrive(0, 1, piece)

        @pl.loop(0, TILES)
        def _(tile):
            for r in range(2):
                at = pl.multiple_of((piece * TILES + tile) * N + r * LANES, LANES)
                here = pl.ds(at, LANES)
                spread = acc[here, :] + x_inverse(0, 1, piece, tile, r)
                spread_re, spread_im = spread[:, :N], spread[:, N:]
                _, _, real_v = medium(at)
                ratio = real_v / damping
                real, imag = spread_re - ratio * spread_im, spread_im + ratio * spread_re
                first[here, 0:N] = real
                first[here, N : 2 * N] = imag
                drive_re = real_v * real + damping * imag + source[here, :]
                drive_im = real_v * imag - damping * real
                for part, value in ((0, drive_re), (1, drive_im)):
                    high, low = split(value)
                    drive_h[here, part * N : (part + 1) * N] = high
                    drive_l[here, part * N : (part + 1) * N] = low
            x_forward(1, 0, piece, tile)

        send(1, 0, piece)
    for piece in range(PIECES):

        @pl.loop(0, TILES)
        def _(tile):
            x_forward(1, 1, piece, tile)

        send(1, 1, piece)

    for half in range(HALVES):
        for piece in range(PIECES):
            arrive(1, half, piece)
        gather(1, half)
        plane[...] = times(plane[...], yh[...], yl[...])
        for member in range(2):
            real, imag = spectrum_z(plane[member * N : (member + 1) * N, :])
            filtered(half, member, real, imag)
        inverse(2, half)
        for piece in range(PIECES):
            send(2, half, piece)

    half_inverse(2)
    loads[11].wait()
    ends = []
    for piece in range(PIECES):
        arrive(2, 1, piece)

        @pl.loop(0, TILES)
        def _(tile):
            for r in range(2):
                at = pl.multiple_of((piece * TILES + tile) * N + r * LANES, LANES)
                here = pl.ds(at, LANES)
                spread = acc[here, :] + x_inverse(2, 1, piece, tile, r)
                was_re, was_im = first[here, 0:N], first[here, N : 2 * N]
                delta_re, delta_im = spread[:, :N] - was_re, spread[:, N:] - was_im
                v, inverse_sq, real_v = medium(at)
                ratio = real_v / damping
                real = was_re + delta_re - ratio * delta_im
                imag = was_im + delta_im + ratio * delta_re
                field[0, here, :] = real
                field[1, here, :] = imag
                misfit = (real - seen[0, here, :]) * real + (imag - seen[1, here, :]) * imag
                part = misfit * (-2.0 * wave_sq) * inverse_sq / v
                term[0, here, :] = jnp.where(core == 0, part[:, :LANES], part[:, LANES:])
                term[1, here, :] = jnp.where(core == 0, part[:, LANES:], part[:, :LANES])

        rows = pl.ds(piece * TILES * N, TILES * N)
        ends.append(
            pltpu.make_async_remote_copy(
                src_ref=term.at[1, rows],
                dst_ref=other.at[rows],
                send_sem=pair_send.at[piece],
                recv_sem=pair_recv.at[piece],
                device_id={"src": 1 - core},
                device_id_type=MESH,
            )
        )
        ends[-1].start()

    for n in range(3 * HALVES * PIECES):
        finish(n, send_sem)
    for piece in range(PIECES):
        ends[piece].wait()


def close(field, term, other, field_out, gradient_out, total, sem):
    put_field = pltpu.make_async_copy(field, field_out, sem.at[0])
    put_field.start()
    total[...] = term[0] + other[...]
    put_total = pltpu.make_async_copy(total, gradient_out, sem.at[1])
    put_total.start()
    put_field.wait()
    put_total.wait()


def per_device(speed, sign_bits, positions, observed):
    f32, bf16 = jnp.float32, jnp.bfloat16
    anywhere = pl.BlockSpec(memory_space=pl.ANY)
    vmem = pl.BlockSpec(memory_space=pltpu.VMEM)
    slots = 3 * HALVES * PIECES
    in_hbm = lambda a: pltpu.with_memory_space_constraint(a, pltpu.HBM)
    field, term, other = pl.pallas_call(
        kernel,
        out_shape=(
            pltpu.VMEM((2, ROWS, N), f32),
            pltpu.VMEM((2, ROWS, LANES), f32),
            pltpu.VMEM((ROWS, LANES), f32),
        ),
        in_specs=[anywhere] * 12,
        out_specs=(vmem, vmem, vmem),
        scratch_shapes=[
            pltpu.VMEM(sign_bits.shape, jnp.int32),
            pltpu.VMEM(positions.shape, jnp.int32),
            pltpu.VMEM((2 * N, 2 * N), bf16),
            pltpu.VMEM((2 * N, 2 * N), bf16),
            pltpu.VMEM((2 * N, N), bf16),
            pltpu.VMEM((2 * N, N), bf16),
            pltpu.VMEM((2 * N, N), bf16),
            pltpu.VMEM((2 * N, N), bf16),
            pltpu.VMEM((2 * N, 2 * N), bf16),
            pltpu.VMEM((2 * N, 2 * N), bf16),
            pltpu.VMEM((slots, CHIPS * MSG, LANES), f32),
            pltpu.VMEM((slots, CHIPS * MSG, LANES), f32),
            pltpu.VMEM((ROWS, 2 * N), f32),
            pltpu.VMEM((ROWS, 2 * N), f32),
            pltpu.VMEM((4, N, 2 * N), f32),
            pltpu.VMEM((2 * N, 2 * N), f32),
            pltpu.VMEM((ROWS, 2 * N), bf16),
            pltpu.VMEM((ROWS, 2 * N), bf16),
            pltpu.VMEM((ROWS, N), f32),
            pltpu.VMEM((ROWS, N), f32),
            pltpu.VMEM((2, ROWS, N), f32),
            pltpu.SemaphoreType.DMA((slots,)),
            pltpu.SemaphoreType.DMA((slots,)),
            pltpu.SemaphoreType.DMA((12,)),
            pltpu.SemaphoreType.DMA((PIECES,)),
            pltpu.SemaphoreType.DMA((PIECES,)),
        ],
        compiler_params=pltpu.CompilerParams(
            collective_id=0, has_side_effects=True, vmem_limit_bytes=44 << 20
        ),
    )(
        in_hbm(speed.reshape(ROWS, N)),
        in_hbm(sign_bits),
        in_hbm(positions),
        in_hbm(observed.reshape(2, ROWS, N)),
        *[in_hbm(jnp.asarray(t)) for t in tables()],
    )
    field, gradient = pl.pallas_call(
        close,
        out_shape=(
            pltpu.HBM((2, ROWS, N), f32),
            pltpu.HBM((ROWS, LANES), f32),
        ),
        in_specs=[anywhere, vmem, vmem],
        out_specs=(anywhere, anywhere),
        scratch_shapes=[
            pltpu.VMEM((ROWS, LANES), f32),
            pltpu.SemaphoreType.DMA((2,)),
        ],
        compiler_params=pltpu.CompilerParams(vmem_limit_bytes=4 << 20),
    )(*[pltpu.with_memory_space_constraint(a, pltpu.VMEM) for a in (field, term, other)])
    return field.reshape(1, 2, BLOCK, BLOCK, N), gradient.reshape(BLOCK, BLOCK, LANES)


def solution(mesh):
    return jax.shard_map(
        per_device,
        mesh=mesh,
        in_specs=(P("pz", "py", None), P("src", None), P(), P("src", None, "pz", "py", None)),
        out_specs=(P("src", None, "pz", "py", None), P("pz", "py", "src")),
        check_vma=False,
    )
```

```python
import functools
import math

import jax
import jax.numpy as jnp
import numpy as np
from jax import lax
from jax.experimental import pallas as pl
from jax.experimental.pallas import tpu as pltpu
from jax.sharding import PartitionSpec as P

MESH = pl.DeviceIdType.MESH
N = 256
SIDE = 8
CHIPS = SIDE * SIDE
BLOCK = N // SIDE
ROWS = BLOCK * BLOCK
LANES = 128
HALVES = 2
PIECES = 2
TILES = 4 // PIECES
MSG = TILES * 8
ORDER = [
    42, 58, 41, 46, 38, 43, 26, 47, 59, 54, 25, 62, 57, 22, 34, 30, 40, 27, 37, 39, 45,
    10, 31, 53, 61, 23, 6, 44, 11, 33, 29, 55, 50, 24, 14, 36, 21, 63, 35, 9, 56, 18,
    51, 13, 20, 60, 17, 7, 49, 8, 19, 28, 2, 52, 5, 32, 15, 3, 16, 48, 4, 1, 12,
]

wave_sq = (2.0 * math.pi / 8.0) ** 2
damping = 0.05
source_gain = 40.0


def tables():
    angle = lambda a, b: 2.0 * np.pi * ((a[:, None] * b[None, :]) % N) / N
    count = np.arange(N)
    chip = np.arange(CHIPS)
    freq = np.stack([2 * chip, (N - 2 * chip) % N, 2 * chip + 1, N - 1 - 2 * chip], 1)
    freq[0, 1] = N // 2
    rows = []
    for half in range(HALVES):
        for member in range(2):
            turn = angle(freq[:, 2 * half + member], count)
            rows.append(np.concatenate([np.cos(turn), np.sin(turn)], 1))
            rows.append(np.concatenate([-np.sin(turn), np.cos(turn)], 1))
    along_x = np.concatenate(rows, 0)
    turn = angle(count, count)
    cosine, sine = np.cos(turn), np.sin(turn)
    along_y = np.block([[cosine, -sine], [sine, cosine]])
    order = z_of_row(count)
    forward = np.concatenate([cosine[:, order], sine[:, order]], 0)
    backward = np.concatenate([cosine[order], sine[order]], 0)
    out = []
    for table in (along_y, forward, backward, along_x):
        high = table.astype(jnp.bfloat16)
        out += [high, (table - high.astype(np.float64)).astype(jnp.bfloat16)]
    return out


def z_of_row(row):
    per = N // PIECES
    piece, rest = row // per, row % per
    s, rest = rest // (16 * TILES), rest % (16 * TILES)
    j, rest = rest // (2 * TILES), rest % (2 * TILES)
    return j * BLOCK + 8 * (piece * TILES) + 4 * rest + s


def split(value):
    high = value.astype(jnp.bfloat16)
    return high, (value - high.astype(jnp.float32)).astype(jnp.bfloat16)


def times(value, high, low):
    first, rest = split(value)
    dot = functools.partial(jnp.dot, preferred_element_type=jnp.float32)
    return dot(first, high) + (dot(first, low) + dot(rest, high))


def times_left(high, low, value):
    first, rest = split(value)
    dot = functools.partial(jnp.dot, preferred_element_type=jnp.float32)
    return dot(high, first) + (dot(low, first) + dot(high, rest))


def swap(parts):
    lane = lax.broadcasted_iota(jnp.int32, parts[0].shape, 1)
    odd, upper = (lane & 32) != 0, (lane & 64) != 0
    mid = []
    for b in (0, 2):
        low, high = parts[b], parts[b + 1]
        mid.append(jnp.where(odd, pltpu.roll(high, 32, 1), low))
        mid.append(jnp.where(odd, high, pltpu.roll(low, 96, 1)))
    out = [None] * 4
    for b in (0, 1):
        low, high = mid[b], mid[b + 2]
        out[b] = jnp.where(upper, pltpu.roll(high, 64, 1), low)
        out[b + 2] = jnp.where(upper, high, pltpu.roll(low, 64, 1))
    return out


def kernel(
    speed_hbm, bits_hbm, pos_hbm, seen_hbm, yh_hbm, yl_hbm, fh_hbm, fl_hbm, bh_hbm, bl_hbm, xh_hbm, xl_hbm,
    field, term, other,
    bits_ref, pos_ref, yh, yl, fh, fl, bh, bl, xh, xl, sent, got, acc, first, green, plane, drive_h, drive_l, source, speed, seen,
    send_sem, recv_sem, load_sem, pair_send, pair_recv,
):
    core, py, pz = lax.axis_index("src"), lax.axis_index("py"), lax.axis_index("pz")
    me = py * SIDE + pz
    X, ZH, Y, ZL = py >> 1, py & 1, pz >> 1, pz & 1
    Z = 2 * ZH + ZL

    def partner(o):
        x, y, z = (X + (o >> 4)) & 3, (Y + ((o >> 2) & 3)) & 3, (Z + (o & 3)) & 3
        return 2 * x + (z >> 1), 2 * y + (z & 1)

    pairs = ((bits_hbm, bits_ref), (pos_hbm, pos_ref), (yh_hbm, yh), (yl_hbm, yl), (fh_hbm, fh), (fl_hbm, fl), (bh_hbm, bh), (bl_hbm, bl),
             (xh_hbm, xh), (xl_hbm, xl), (speed_hbm, speed), (seen_hbm, seen))
    loads = [pltpu.make_async_copy(a, b, load_sem.at[n]) for n, (a, b) in enumerate(pairs)]
    for load in loads[:2]:
        load.start()
    barrier = pltpu.get_barrier_semaphore()

    for o in ORDER:
        a, b = partner(o)
        pl.semaphore_signal(barrier, inc=1, device_id={"py": a, "pz": b}, device_id_type=MESH)

    pl.semaphore_signal(barrier, inc=1, device_id={"src": 1 - core}, device_id_type=MESH)

    for load in loads[2:]:
        load.start()

    def slot(phase, half, piece):
        return (phase * HALVES + half) * PIECES + piece

    def send(phase, half, piece):
        n = slot(phase, half, piece)
        mine = pl.ds(pl.multiple_of(me * MSG, MSG), MSG)

        for o in ORDER:
            a, b = partner(o)
            theirs = pl.ds(pl.multiple_of((a * SIDE + b) * MSG, MSG), MSG)
            pltpu.make_async_remote_copy(
                src_ref=sent.at[n, theirs],
                dst_ref=got.at[n, mine],
                send_sem=send_sem.at[n],
                recv_sem=recv_sem.at[n],
                device_id={"py": a, "pz": b},
                device_id_type=MESH,
            ).start()

        got[n, mine] = sent[n, mine]

    def finish(n, sem):
        everyone = got.at[n, pl.ds(0, (CHIPS - 1) * MSG)]
        pltpu.make_async_copy(everyone, everyone, sem.at[n]).wait()

    def arrive(phase, half, piece):
        finish(slot(phase, half, piece), recv_sem)

    def wave_of(index):
        signed = jnp.where(index < N // 2, index, index - N)
        return signed.astype(jnp.float32) * (2.0 * math.pi / N)

    row_id = lax.broadcasted_iota(jnp.int32, (N, N), 0)
    lane_id = lax.broadcasted_iota(jnp.int32, (N, N), 1)
    base = wave_of(row_id) ** 2 + wave_of(lane_id) ** 2

    def green_of(half, member):
        index = 2 * me + half
        if half == 0 and member == 1:
            index = jnp.where(me == 0, N // 2, index)
        wave = index.astype(jnp.float32) * (2.0 * math.pi / N)
        shifted = base + wave * wave - wave_sq
        scale = (1.0 / N**3) / (shifted * shifted + damping * damping)
        green[2 * half + member, :, 0:N] = shifted * scale
        green[2 * half + member, :, N : 2 * N] = damping * scale

    def spectrum_z(value):
        both = times_left(fh[...], fl[...], value)
        real = both[:N, :N] + both[N:, N:]
        imag = both[:N, N:] - both[N:, :N]
        return real, imag

    def filtered(half, member, real, imag):
        g_re = green[2 * half + member, :, 0:N]
        g_im = green[2 * half + member, :, N : 2 * N]
        plane[member * N : (member + 1) * N, 0:N] = real * g_im + imag * g_re
        plane[member * N : (member + 1) * N, N : 2 * N] = real * g_re - imag * g_im

    def inverse(phase, half):
        plane[...] = times(plane[...], yh[...], yl[...])
        for member in range(2):
            both = times_left(bh[...], bl[...], plane[member * N : (member + 1) * N, :])
            real = both[:N, N:] - both[N:, :N]
            imag = both[:N, :N] + both[N:, N:]
            size = 16 * TILES
            for part, value in ((0, real), (1, imag)):
                for piece in range(PIECES):
                    n = slot(phase, half, piece)
                    for h in range(2):
                        rows = [
                            value[(piece * 4 + s) * size : (piece * 4 + s + 1) * size, h * LANES : (h + 1) * LANES]
                            for s in range(4)
                        ]
                        for b, block in enumerate(swap(rows)):
                            start = (4 * h + b) * SIDE * MSG + 2 * member + part
                            sent[n, pl.ds(start, size, stride=4), :] = block

    def gather(phase, half):
        size = 16 * TILES
        for piece in range(PIECES):
            n = slot(phase, half, piece)
            for member in range(2):
                for part in range(2):
                    for h in range(2):
                        rows = [
                            got[n, pl.ds((4 * h + b) * SIDE * MSG + 2 * member + part, size, stride=4), :]
                            for b in range(4)
                        ]
                        for s, block in enumerate(swap(rows)):
                            at = member * N + (piece * 4 + s) * size
                            plane[at : at + size, part * N + h * LANES : part * N + (h + 1) * LANES] = block

    for load in loads[:2]:
        load.wait()
    weight = (2 * bits_ref[...] - 1).astype(jnp.float32) * source_gain
    emitters = weight.shape[1]
    z_at, y_at, x_at = pos_ref[0:1, :], pos_ref[1:2, :], pos_ref[2:3, :]
    ids = lax.broadcasted_iota(jnp.int32, (N, emitters), 0)

    def hits(where, index):
        return jnp.where(where == index, 1.0, 0.0).astype(jnp.bfloat16)

    which = lax.broadcasted_iota(jnp.int32, (8, N), 0)
    turn = lax.broadcasted_iota(jnp.int32, (8, N), 1)
    only = jnp.logical_and(which == 1, me == 0)
    turn = (turn * jnp.where(only, N // 2, 2 * me + which // 2)) & (N - 1)
    shift = jnp.where(jnp.logical_and(which % 2 == 1, jnp.logical_not(only)), math.pi / 2.0, 0.0)
    wave_rows = jnp.cos(turn.astype(jnp.float32) * (2.0 * math.pi / N) - shift)
    wh, wl = split(wave_rows)
    x_hits = hits(x_at, ids)
    phases = jnp.dot(wh, x_hits, preferred_element_type=jnp.float32) + jnp.dot(
        wl, x_hits, preferred_element_type=jnp.float32
    )
    phases = phases * weight
    y_hits = hits(y_at, ids)
    z_equal = z_at == z_of_row(ids)

    nt = (((1,), (1,)), ((), ()))
    for half in range(HALVES):
        for member in range(2):
            row = phases[2 * half + member : 2 * half + member + 1, :]
            high = row.astype(jnp.bfloat16).astype(jnp.float32)
            value = 0.0
            for piece_row in (high, row - high):
                left = jnp.where(z_equal, piece_row, 0.0).astype(jnp.bfloat16)
                value = value + lax.dot_general(left, y_hits, nt, preferred_element_type=jnp.float32)
            plane[member * N : (member + 1) * N, 0:N] = value
        if half == 0:
            for load in loads[2:8]:
                load.wait()
        lines = times(plane[:, 0:N], yh[0:N, :], yl[0:N, :])
        one_re, one_im = spectrum_z(lines[:N])
        two_re, two_im = spectrum_z(lines[N:])
        for member in range(2):
            green_of(half, member)
        plus_re, plus_im = one_re + two_im, one_im - two_re
        minus_re, minus_im = one_re - two_im, one_im + two_re
        if half == 0:
            alone = me == 0
            plus_re, plus_im = jnp.where(alone, one_re, plus_re), jnp.where(alone, one_im, plus_im)
            minus_re, minus_im = jnp.where(alone, two_re, minus_re), jnp.where(alone, two_im, minus_im)
        filtered(half, 0, plus_re, plus_im)
        filtered(half, 1, minus_re, minus_im)
        inverse(0, half)
        if half == 0:
            pl.semaphore_wait(barrier, CHIPS)
        for piece in range(PIECES):
            send(0, half, piece)

    local_z, local_y = z_at - pz * BLOCK, y_at - py * BLOCK
    inside = (local_z >= 0) & (local_z < BLOCK) & (local_y >= 0) & (local_y < BLOCK)
    cell = jnp.where(inside, local_z * BLOCK + local_y, -1)
    lines = jnp.where(x_at == ids, weight, 0.0).astype(jnp.bfloat16)

    @pl.loop(0, ROWS // N)
    def _(g):
        at = pl.multiple_of(g * N, N)
        source[pl.ds(at, N), :] = lax.dot_general(
            hits(cell - at, ids), lines, nt, preferred_element_type=jnp.float32
        )

    for load in loads[8:11]:
        load.wait()

    def x_inverse(phase, half, piece, tile, r):
        n = slot(phase, half, piece)
        rows = [got[n, pl.ds(tile * 8 + r * 4 + kc, CHIPS, stride=MSG), :] for kc in range(4)]
        return times(jnp.concatenate(rows, 0).T, xh[half * N : (half + 1) * N, :], xl[half * N : (half + 1) * N, :])

    def x_forward(phase, half, piece, tile):
        n = slot(phase, half, piece)
        at = pl.multiple_of((piece * TILES + tile) * N, N)
        high, low = drive_h[pl.ds(at, N), :], drive_l[pl.ds(at, N), :]
        table_h, table_l = xh[half * N : (half + 1) * N, :], xl[half * N : (half + 1) * N, :]
        dot = lambda a, b: lax.dot_general(a, b, nt, preferred_element_type=jnp.float32)
        out = dot(table_h, high) + (dot(table_l, high) + dot(table_h, low))
        for r in range(2):
            for kc in range(4):
                sent[n, pl.ds(tile * 8 + r * 4 + kc, CHIPS, stride=MSG), :] = out[
                    kc * CHIPS : (kc + 1) * CHIPS, r * LANES : (r + 1) * LANES
                ]

    def half_inverse(phase):
        for piece in range(PIECES):
            arrive(phase, 0, piece)

            @pl.loop(0, TILES)
            def _(tile):
                for r in range(2):
                    at = pl.multiple_of((piece * TILES + tile) * N + r * LANES, LANES)
                    acc[pl.ds(at, LANES), :] = x_inverse(phase, 0, piece, tile, r)

    def medium(at):
        v = speed[pl.ds(at, LANES), :]
        inverse_sq = 1.0 / (v * v)
        real_v = wave_sq * (inverse_sq - 1.0)
        return v, inverse_sq, real_v

    half_inverse(0)
    for piece in range(PIECES):
        arrive(0, 1, piece)

        @pl.loop(0, TILES)
        def _(tile):
            for r in range(2):
                at = pl.multiple_of((piece * TILES + tile) * N + r * LANES, LANES)
                here = pl.ds(at, LANES)
                spread = acc[here, :] + x_inverse(0, 1, piece, tile, r)
                spread_re, spread_im = spread[:, :N], spread[:, N:]
                _, _, real_v = medium(at)
                ratio = real_v / damping
                real, imag = spread_re - ratio * spread_im, spread_im + ratio * spread_re
                first[here, 0:N] = real
                first[here, N : 2 * N] = imag
                drive_re = real_v * real + damping * imag + source[here, :]
                drive_im = real_v * imag - damping * real
                for part, value in ((0, drive_re), (1, drive_im)):
                    high, low = split(value)
                    drive_h[here, part * N : (part + 1) * N] = high
                    drive_l[here, part * N : (part + 1) * N] = low
            x_forward(1, 0, piece, tile)

        send(1, 0, piece)
    for piece in range(PIECES):

        @pl.loop(0, TILES)
        def _(tile):
            x_forward(1, 1, piece, tile)

        send(1, 1, piece)

    for half in range(HALVES):
        for piece in range(PIECES):
            arrive(1, half, piece)
        gather(1, half)
        plane[...] = times(plane[...], yh[...], yl[...])
        for member in range(2):
            real, imag = spectrum_z(plane[member * N : (member + 1) * N, :])
            filtered(half, member, real, imag)
        inverse(2, half)
        for piece in range(PIECES):
            send(2, half, piece)

    half_inverse(2)
    loads[11].wait()
    ends = []
    for piece in range(PIECES):
        arrive(2, 1, piece)

        @pl.loop(0, TILES)
        def _(tile):
            for r in range(2):
                at = pl.multiple_of((piece * TILES + tile) * N + r * LANES, LANES)
                here = pl.ds(at, LANES)
                spread = acc[here, :] + x_inverse(2, 1, piece, tile, r)
                was_re, was_im = first[here, 0:N], first[here, N : 2 * N]
                delta_re, delta_im = spread[:, :N] - was_re, spread[:, N:] - was_im
                v, inverse_sq, real_v = medium(at)
                ratio = real_v / damping
                real = was_re + delta_re - ratio * delta_im
                imag = was_im + delta_im + ratio * delta_re
                field[0, here, :] = real
                field[1, here, :] = imag
                misfit = (real - seen[0, here, :]) * real + (imag - seen[1, here, :]) * imag
                part = misfit * (-2.0 * wave_sq) * inverse_sq / v
                term[0, here, :] = jnp.where(core == 0, part[:, :LANES], part[:, LANES:])
                term[1, here, :] = jnp.where(core == 0, part[:, LANES:], part[:, :LANES])

        rows = pl.ds(piece * TILES * N, TILES * N)
        ends.append(
            pltpu.make_async_remote_copy(
                src_ref=term.at[1, rows],
                dst_ref=other.at[rows],
                send_sem=pair_send.at[piece],
                recv_sem=pair_recv.at[piece],
                device_id={"src": 1 - core},
                device_id_type=MESH,
            )
        )
        ends[-1].start()

    for n in range(3 * HALVES * PIECES):
        finish(n, send_sem)
    for piece in range(PIECES):
        ends[piece].wait()


def close(field, term, other, field_out, gradient_out, total, sem):
    put_field = pltpu.make_async_copy(field, field_out, sem.at[0])
    put_field.start()
    total[...] = term[0] + other[...]
    put_total = pltpu.make_async_copy(total, gradient_out, sem.at[1])
    put_total.start()
    put_field.wait()
    put_total.wait()


def per_device(speed, sign_bits, positions, observed):
    f32, bf16 = jnp.float32, jnp.bfloat16
    anywhere = pl.BlockSpec(memory_space=pl.ANY)
    vmem = pl.BlockSpec(memory_space=pltpu.VMEM)
    slots = 3 * HALVES * PIECES
    in_hbm = lambda a: pltpu.with_memory_space_constraint(a, pltpu.HBM)
    field, term, other = pl.pallas_call(
        kernel,
        out_shape=(
            pltpu.VMEM((2, ROWS, N), f32),
            pltpu.VMEM((2, ROWS, LANES), f32),
            pltpu.VMEM((ROWS, LANES), f32),
        ),
        in_specs=[anywhere] * 12,
        out_specs=(vmem, vmem, vmem),
        scratch_shapes=[
            pltpu.VMEM(sign_bits.shape, jnp.int32),
            pltpu.VMEM(positions.shape, jnp.int32),
            pltpu.VMEM((2 * N, 2 * N), bf16),
            pltpu.VMEM((2 * N, 2 * N), bf16),
            pltpu.VMEM((2 * N, N), bf16),
            pltpu.VMEM((2 * N, N), bf16),
            pltpu.VMEM((2 * N, N), bf16),
            pltpu.VMEM((2 * N, N), bf16),
            pltpu.VMEM((2 * N, 2 * N), bf16),
            pltpu.VMEM((2 * N, 2 * N), bf16),
            pltpu.VMEM((slots, CHIPS * MSG, LANES), f32),
            pltpu.VMEM((slots, CHIPS * MSG, LANES), f32),
            pltpu.VMEM((ROWS, 2 * N), f32),
            pltpu.VMEM((ROWS, 2 * N), f32),
            pltpu.VMEM((4, N, 2 * N), f32),
            pltpu.VMEM((2 * N, 2 * N), f32),
            pltpu.VMEM((ROWS, 2 * N), bf16),
            pltpu.VMEM((ROWS, 2 * N), bf16),
            pltpu.VMEM((ROWS, N), f32),
            pltpu.VMEM((ROWS, N), f32),
            pltpu.VMEM((2, ROWS, N), f32),
            pltpu.SemaphoreType.DMA((slots,)),
            pltpu.SemaphoreType.DMA((slots,)),
            pltpu.SemaphoreType.DMA((12,)),
            pltpu.SemaphoreType.DMA((PIECES,)),
            pltpu.SemaphoreType.DMA((PIECES,)),
        ],
        compiler_params=pltpu.CompilerParams(
            collective_id=0, has_side_effects=True, vmem_limit_bytes=44 << 20
        ),
    )(
        in_hbm(speed.reshape(ROWS, N)),
        in_hbm(sign_bits),
        in_hbm(positions),
        in_hbm(observed.reshape(2, ROWS, N)),
        *[in_hbm(jnp.asarray(t)) for t in tables()],
    )
    field, gradient = pl.pallas_call(
        close,
        out_shape=(
            pltpu.HBM((2, ROWS, N), f32),
            pltpu.HBM((ROWS, LANES), f32),
        ),
        in_specs=[anywhere, vmem, vmem],
        out_specs=(anywhere, anywhere),
        scratch_shapes=[
            pltpu.VMEM((ROWS, LANES), f32),
            pltpu.SemaphoreType.DMA((2,)),
        ],
        compiler_params=pltpu.CompilerParams(vmem_limit_bytes=4 << 20),
    )(*[pltpu.with_memory_space_constraint(a, pltpu.VMEM) for a in (field, term, other)])
    return field.reshape(1, 2, BLOCK, BLOCK, N), gradient.reshape(BLOCK, BLOCK, LANES)


def solution(mesh):
    return jax.shard_map(
        per_device,
        mesh=mesh,
        in_specs=(P("pz", "py", None), P("src", None), P(), P("src", None, "pz", "py", None)),
        out_specs=(P("src", None, "pz", "py", None), P("pz", "py", "src")),
        check_vma=False,
    )
```

```python
import functools
import math

import jax
import jax.numpy as jnp
import numpy as np
from jax import lax
from jax.experimental import pallas as pl
from jax.experimental.pallas import tpu as pltpu
from jax.sharding import PartitionSpec as P

MESH = pl.DeviceIdType.MESH
N = 256
SIDE = 8
CHIPS = SIDE * SIDE
BLOCK = N // SIDE
ROWS = BLOCK * BLOCK
LANES = 128
HALVES = 2
PIECES = 2
TILES = 4 // PIECES
MSG = TILES * 8
ORDER = [
    42, 58, 41, 46, 38, 43, 26, 47, 59, 54, 25, 62, 57, 22, 34, 30, 40, 27, 37, 39, 45,
    10, 31, 53, 61, 23, 6, 44, 11, 33, 29, 55, 50, 24, 14, 36, 21, 63, 35, 9, 56, 18,
    51, 13, 20, 60, 17, 7, 49, 8, 19, 28, 2, 52, 5, 32, 15, 3, 16, 48, 4, 1, 12,
]

wave_sq = (2.0 * math.pi / 8.0) ** 2
damping = 0.05
source_gain = 40.0


def tables():
    angle = lambda a, b: 2.0 * np.pi * ((a[:, None] * b[None, :]) % N) / N
    count = np.arange(N)
    chip = np.arange(CHIPS)
    freq = np.stack([2 * chip + 1, N - 1 - 2 * chip, 2 * chip, (N - 2 * chip) % N], 1)
    freq[0, 3] = N // 2
    rows = []
    for half in range(HALVES):
        for member in range(2):
            turn = angle(freq[:, 2 * half + member], count)
            rows.append(np.concatenate([np.cos(turn), np.sin(turn)], 1))
            rows.append(np.concatenate([-np.sin(turn), np.cos(turn)], 1))
    along_x = np.concatenate(rows, 0)
    turn = angle(count, count)
    cosine, sine = np.cos(turn), np.sin(turn)
    along_y = np.block([[cosine, -sine], [sine, cosine]])
    order = z_of_row(count)
    forward = np.concatenate([cosine[:, order], sine[:, order]], 0)
    backward = np.concatenate([cosine[order], sine[order]], 0)
    out = []
    for table in (along_y, forward, backward, along_x):
        high = table.astype(jnp.bfloat16)
        out += [high, (table - high.astype(np.float64)).astype(jnp.bfloat16)]
    return out


def z_of_row(row):
    per = N // PIECES
    piece, rest = row // per, row % per
    s, rest = rest // (16 * TILES), rest % (16 * TILES)
    j, rest = rest // (2 * TILES), rest % (2 * TILES)
    return j * BLOCK + 8 * (piece * TILES) + 4 * rest + s


def split(value):
    high = value.astype(jnp.bfloat16)
    return high, (value - high.astype(jnp.float32)).astype(jnp.bfloat16)


def times(value, high, low):
    first, rest = split(value)
    dot = functools.partial(jnp.dot, preferred_element_type=jnp.float32)
    return dot(first, high) + (dot(first, low) + dot(rest, high))


def times_left(high, low, value):
    first, rest = split(value)
    dot = functools.partial(jnp.dot, preferred_element_type=jnp.float32)
    return dot(high, first) + (dot(low, first) + dot(high, rest))


def swap(parts):
    lane = lax.broadcasted_iota(jnp.int32, parts[0].shape, 1)
    odd, upper = (lane & 32) != 0, (lane & 64) != 0
    mid = []
    for b in (0, 2):
        low, high = parts[b], parts[b + 1]
        mid.append(jnp.where(odd, pltpu.roll(high, 32, 1), low))
        mid.append(jnp.where(odd, high, pltpu.roll(low, 96, 1)))
    out = [None] * 4
    for b in (0, 1):
        low, high = mid[b], mid[b + 2]
        out[b] = jnp.where(upper, pltpu.roll(high, 64, 1), low)
        out[b + 2] = jnp.where(upper, high, pltpu.roll(low, 64, 1))
    return out


def kernel(
    speed_hbm, bits_hbm, pos_hbm, seen_hbm, yh_hbm, yl_hbm, fh_hbm, fl_hbm, bh_hbm, bl_hbm, xh_hbm, xl_hbm,
    field, term, other,
    bits_ref, pos_ref, yh, yl, fh, fl, bh, bl, xh, xl, sent, got, acc, first, green, plane, drive_h, drive_l, source, speed, seen,
    send_sem, recv_sem, load_sem, pair_send, pair_recv,
):
    core, py, pz = lax.axis_index("src"), lax.axis_index("py"), lax.axis_index("pz")
    me = py * SIDE + pz
    X, ZH, Y, ZL = py >> 1, py & 1, pz >> 1, pz & 1
    Z = 2 * ZH + ZL

    def partner(o):
        x, y, z = (X + (o >> 4)) & 3, (Y + ((o >> 2) & 3)) & 3, (Z + (o & 3)) & 3
        return 2 * x + (z >> 1), 2 * y + (z & 1)

    pairs = ((bits_hbm, bits_ref), (pos_hbm, pos_ref), (yh_hbm, yh), (yl_hbm, yl), (fh_hbm, fh), (fl_hbm, fl), (bh_hbm, bh), (bl_hbm, bl),
             (xh_hbm, xh), (xl_hbm, xl), (speed_hbm, speed), (seen_hbm, seen))
    loads = [pltpu.make_async_copy(a, b, load_sem.at[n]) for n, (a, b) in enumerate(pairs)]
    for load in loads[:2]:
        load.start()
    barrier = pltpu.get_barrier_semaphore()

    for o in ORDER:
        a, b = partner(o)
        pl.semaphore_signal(barrier, inc=1, device_id={"py": a, "pz": b}, device_id_type=MESH)

    pl.semaphore_signal(barrier, inc=1, device_id={"src": 1 - core}, device_id_type=MESH)

    for load in loads[2:]:
        load.start()

    def slot(phase, half, piece):
        return (phase * HALVES + half) * PIECES + piece

    def send(phase, half, piece):
        n = slot(phase, half, piece)
        mine = pl.ds(pl.multiple_of(me * MSG, MSG), MSG)

        for o in ORDER:
            a, b = partner(o)
            theirs = pl.ds(pl.multiple_of((a * SIDE + b) * MSG, MSG), MSG)
            pltpu.make_async_remote_copy(
                src_ref=sent.at[n, theirs],
                dst_ref=got.at[n, mine],
                send_sem=send_sem.at[n],
                recv_sem=recv_sem.at[n],
                device_id={"py": a, "pz": b},
                device_id_type=MESH,
            ).start()

        got[n, mine] = sent[n, mine]

    def finish(n, sem):
        everyone = got.at[n, pl.ds(0, (CHIPS - 1) * MSG)]
        pltpu.make_async_copy(everyone, everyone, sem.at[n]).wait()

    def arrive(phase, half, piece):
        finish(slot(phase, half, piece), recv_sem)

    def wave_of(index):
        signed = jnp.where(index < N // 2, index, index - N)
        return signed.astype(jnp.float32) * (2.0 * math.pi / N)

    row_id = lax.broadcasted_iota(jnp.int32, (N, N), 0)
    lane_id = lax.broadcasted_iota(jnp.int32, (N, N), 1)
    base = wave_of(row_id) ** 2 + wave_of(lane_id) ** 2

    def green_of(half, member):
        index = 2 * me + 1 - half
        if half == 1 and member == 1:
            index = jnp.where(me == 0, N // 2, index)
        wave = index.astype(jnp.float32) * (2.0 * math.pi / N)
        shifted = base + wave * wave - wave_sq
        scale = (1.0 / N**3) / (shifted * shifted + damping * damping)
        green[2 * half + member, :, 0:N] = shifted * scale
        green[2 * half + member, :, N : 2 * N] = damping * scale

    def spectrum_z(value):
        both = times_left(fh[...], fl[...], value)
        real = both[:N, :N] + both[N:, N:]
        imag = both[:N, N:] - both[N:, :N]
        return real, imag

    def filtered(half, member, real, imag):
        g_re = green[2 * half + member, :, 0:N]
        g_im = green[2 * half + member, :, N : 2 * N]
        plane[member * N : (member + 1) * N, 0:N] = real * g_im + imag * g_re
        plane[member * N : (member + 1) * N, N : 2 * N] = real * g_re - imag * g_im

    def inverse_pieces(phase, half, pieces, conjugate):
        size = 16 * TILES
        high = 4 * size
        if len(pieces) == PIECES:
            table_h, table_l = bh[...], bl[...]
        else:
            at = pieces[0] * high
            table_h = jnp.concatenate([bh[at : at + high, :], bh[N + at : N + at + high, :]], 0)
            table_l = jnp.concatenate([bl[at : at + high, :], bl[N + at : N + at + high, :]], 0)
        high = high * len(pieces)
        for member in range(2):
            both = times_left(table_h, table_l, plane[member * N : (member + 1) * N, :])
            real = both[:high, N:] - both[high:, :N]
            imag = both[:high, :N] + both[high:, N:]
            if conjugate and member == 0:
                imag = -imag
            for part, value in ((0, real), (1, imag)):
                for place, piece in enumerate(pieces):
                    n = slot(phase, half, piece)
                    for h in range(2):
                        rows = [
                            value[(place * 4 + s) * size : (place * 4 + s + 1) * size, h * LANES : (h + 1) * LANES]
                            for s in range(4)
                        ]
                        for b, block in enumerate(swap(rows)):
                            start = (4 * h + b) * SIDE * MSG + 2 * member + part
                            sent[n, pl.ds(start, size, stride=4), :] = block

    def inverse(phase, half):
        plane[...] = times(plane[...], yh[...], yl[...])
        inverse_pieces(phase, half, range(PIECES), False)

    def gather(phase, half):
        size = 16 * TILES
        for piece in range(PIECES):
            n = slot(phase, half, piece)
            for member in range(2):
                for part in range(2):
                    for h in range(2):
                        rows = [
                            got[n, pl.ds((4 * h + b) * SIDE * MSG + 2 * member + part, size, stride=4), :]
                            for b in range(4)
                        ]
                        for s, block in enumerate(swap(rows)):
                            at = member * N + (piece * 4 + s) * size
                            plane[at : at + size, part * N + h * LANES : part * N + (h + 1) * LANES] = block

    for load in loads[:2]:
        load.wait()
    weight = (2 * bits_ref[...] - 1).astype(jnp.float32) * source_gain
    emitters = weight.shape[1]
    z_at, y_at, x_at = pos_ref[0:1, :], pos_ref[1:2, :], pos_ref[2:3, :]
    ids = lax.broadcasted_iota(jnp.int32, (N, emitters), 0)

    def hits(where, index):
        return jnp.where(where == index, 1.0, 0.0).astype(jnp.bfloat16)

    which = lax.broadcasted_iota(jnp.int32, (8, N), 0)
    turn = lax.broadcasted_iota(jnp.int32, (8, N), 1)
    only = jnp.logical_and(which == 3, me == 0)
    turn = (turn * jnp.where(only, N // 2, 2 * me + jnp.where(which < 2, 1, 0))) & (N - 1)
    shift = jnp.where(jnp.logical_and(which % 2 == 1, jnp.logical_not(only)), math.pi / 2.0, 0.0)
    wave_rows = jnp.cos(turn.astype(jnp.float32) * (2.0 * math.pi / N) - shift)
    wh, wl = split(wave_rows)
    x_hits = hits(x_at, ids)
    phases = jnp.dot(wh, x_hits, preferred_element_type=jnp.float32) + jnp.dot(
        wl, x_hits, preferred_element_type=jnp.float32
    )
    phases = phases * weight
    y_hits = hits(y_at, ids)
    z_equal = z_at == z_of_row(ids)

    nt = (((1,), (1,)), ((), ()))
    for half in range(HALVES):
        for member in range(2):
            row = phases[2 * half + member : 2 * half + member + 1, :]
            high = row.astype(jnp.bfloat16).astype(jnp.float32)
            value = 0.0
            for piece_row in (high, row - high):
                left = jnp.where(z_equal, piece_row, 0.0).astype(jnp.bfloat16)
                value = value + lax.dot_general(left, y_hits, nt, preferred_element_type=jnp.float32)
            if half == 0:
                plane[0:N, member * N : (member + 1) * N] = value
            else:
                plane[member * N : (member + 1) * N, 0:N] = value
        for member in range(2):
            green_of(half, member)
        if half == 0:
            for load in loads[2:8]:
                load.wait()
            real, imag = spectrum_z(times(plane[0:N, :], yh[...], yl[...]))
            g_re, g_im = green[0, :, 0:N], green[0, :, N : 2 * N]
            rr, ii, ri, ir = real * g_re, imag * g_im, real * g_im, imag * g_re
            plane[0:N, 0:N], plane[0:N, N : 2 * N] = ir - ri, rr + ii
            plane[N : 2 * N, 0:N], plane[N : 2 * N, N : 2 * N] = ir + ri, rr - ii
            plane[...] = times(plane[...], yh[...], yl[...])
            for piece in range(PIECES):
                inverse_pieces(0, 0, [piece], True)
                if piece == 0:
                    pl.semaphore_wait(barrier, CHIPS)
                send(0, 0, piece)
        else:
            lines = times(plane[:, 0:N], yh[0:N, :], yl[0:N, :])
            one_re, one_im = spectrum_z(lines[:N])
            two_re, two_im = spectrum_z(lines[N:])
            alone = me == 0
            filtered(1, 0, jnp.where(alone, one_re, one_re + two_im), jnp.where(alone, one_im, one_im - two_re))
            filtered(1, 1, jnp.where(alone, two_re, one_re - two_im), jnp.where(alone, two_im, one_im + two_re))
            inverse(0, 1)
            for piece in range(PIECES):
                send(0, 1, piece)

    local_z, local_y = z_at - pz * BLOCK, y_at - py * BLOCK
    inside = (local_z >= 0) & (local_z < BLOCK) & (local_y >= 0) & (local_y < BLOCK)
    cell = jnp.where(inside, local_z * BLOCK + local_y, -1)
    lines = jnp.where(x_at == ids, weight, 0.0).astype(jnp.bfloat16)

    @pl.loop(0, ROWS // N)
    def _(g):
        at = pl.multiple_of(g * N, N)
        source[pl.ds(at, N), :] = lax.dot_general(
            hits(cell - at, ids), lines, nt, preferred_element_type=jnp.float32
        )

    for load in loads[8:11]:
        load.wait()

    def x_inverse(phase, half, piece, tile, r):
        n = slot(phase, half, piece)
        rows = [got[n, pl.ds(tile * 8 + r * 4 + kc, CHIPS, stride=MSG), :] for kc in range(4)]
        return times(jnp.concatenate(rows, 0).T, xh[half * N : (half + 1) * N, :], xl[half * N : (half + 1) * N, :])

    def x_forward(phase, half, piece, tile):
        n = slot(phase, half, piece)
        at = pl.multiple_of((piece * TILES + tile) * N, N)
        high, low = drive_h[pl.ds(at, N), :], drive_l[pl.ds(at, N), :]
        table_h, table_l = xh[half * N : (half + 1) * N, :], xl[half * N : (half + 1) * N, :]
        dot = lambda a, b: lax.dot_general(a, b, nt, preferred_element_type=jnp.float32)
        out = dot(table_h, high) + (dot(table_l, high) + dot(table_h, low))
        for r in range(2):
            for kc in range(4):
                sent[n, pl.ds(tile * 8 + r * 4 + kc, CHIPS, stride=MSG), :] = out[
                    kc * CHIPS : (kc + 1) * CHIPS, r * LANES : (r + 1) * LANES
                ]

    def half_inverse(phase):
        for piece in range(PIECES):
            arrive(phase, 0, piece)

            @pl.loop(0, TILES)
            def _(tile):
                for r in range(2):
                    at = pl.multiple_of((piece * TILES + tile) * N + r * LANES, LANES)
                    acc[pl.ds(at, LANES), :] = x_inverse(phase, 0, piece, tile, r)

    def medium(at):
        v = speed[pl.ds(at, LANES), :]
        inverse_sq = 1.0 / (v * v)
        real_v = wave_sq * (inverse_sq - 1.0)
        return v, inverse_sq, real_v

    half_inverse(0)
    for piece in range(PIECES):
        arrive(0, 1, piece)

        @pl.loop(0, TILES)
        def _(tile):
            for r in range(2):
                at = pl.multiple_of((piece * TILES + tile) * N + r * LANES, LANES)
                here = pl.ds(at, LANES)
                spread = acc[here, :] + x_inverse(0, 1, piece, tile, r)
                spread_re, spread_im = spread[:, :N], spread[:, N:]
                _, _, real_v = medium(at)
                ratio = real_v / damping
                real, imag = spread_re - ratio * spread_im, spread_im + ratio * spread_re
                first[here, 0:N] = real
                first[here, N : 2 * N] = imag
                drive_re = real_v * real + damping * imag + source[here, :]
                drive_im = real_v * imag - damping * real
                for part, value in ((0, drive_re), (1, drive_im)):
                    high, low = split(value)
                    drive_h[here, part * N : (part + 1) * N] = high
                    drive_l[here, part * N : (part + 1) * N] = low
            x_forward(1, 0, piece, tile)

        send(1, 0, piece)
    for piece in range(PIECES):

        @pl.loop(0, TILES)
        def _(tile):
            x_forward(1, 1, piece, tile)

        send(1, 1, piece)

    for half in range(HALVES):
        for piece in range(PIECES):
            arrive(1, half, piece)
        gather(1, half)
        plane[...] = times(plane[...], yh[...], yl[...])
        for member in range(2):
            real, imag = spectrum_z(plane[member * N : (member + 1) * N, :])
            filtered(half, member, real, imag)
        inverse(2, half)
        for piece in range(PIECES):
            send(2, half, piece)

    half_inverse(2)
    loads[11].wait()

    def tell(n):
        rows = pl.ds(pl.multiple_of(n * N, N), N)
        return pltpu.make_async_remote_copy(
            src_ref=term.at[1, rows],
            dst_ref=other.at[rows],
            send_sem=pair_send.at[n],
            recv_sem=pair_recv.at[n],
            device_id={"src": 1 - core},
            device_id_type=MESH,
        )

    for piece in range(PIECES):
        arrive(2, 1, piece)

        @pl.loop(0, TILES)
        def _(tile):
            for r in range(2):
                at = pl.multiple_of((piece * TILES + tile) * N + r * LANES, LANES)
                here = pl.ds(at, LANES)
                spread = acc[here, :] + x_inverse(2, 1, piece, tile, r)
                was_re, was_im = first[here, 0:N], first[here, N : 2 * N]
                delta_re, delta_im = spread[:, :N] - was_re, spread[:, N:] - was_im
                v, inverse_sq, real_v = medium(at)
                ratio = real_v / damping
                real = was_re + delta_re - ratio * delta_im
                imag = was_im + delta_im + ratio * delta_re
                field[0, here, :] = real
                field[1, here, :] = imag
                misfit = (real - seen[0, here, :]) * real + (imag - seen[1, here, :]) * imag
                part = misfit * (-2.0 * wave_sq) * inverse_sq / v
                term[0, here, :] = jnp.where(core == 0, part[:, :LANES], part[:, LANES:])
                term[1, here, :] = jnp.where(core == 0, part[:, LANES:], part[:, :LANES])

            tell(piece * TILES + tile).start()

    for n in range(3 * HALVES * PIECES):
        finish(n, send_sem)
    for n in range(ROWS // N):
        tell(n).wait()


def close(field, term, other, field_out, gradient_out, total, sem):
    put_field = pltpu.make_async_copy(field, field_out, sem.at[0])
    put_field.start()
    total[...] = term[0] + other[...]
    put_total = pltpu.make_async_copy(total, gradient_out, sem.at[1])
    put_total.start()
    put_field.wait()
    put_total.wait()


def per_device(speed, sign_bits, positions, observed):
    f32, bf16 = jnp.float32, jnp.bfloat16
    anywhere = pl.BlockSpec(memory_space=pl.ANY)
    vmem = pl.BlockSpec(memory_space=pltpu.VMEM)
    slots = 3 * HALVES * PIECES
    in_hbm = lambda a: pltpu.with_memory_space_constraint(a, pltpu.HBM)
    field, term, other = pl.pallas_call(
        kernel,
        out_shape=(
            pltpu.VMEM((2, ROWS, N), f32),
            pltpu.VMEM((2, ROWS, LANES), f32),
            pltpu.VMEM((ROWS, LANES), f32),
        ),
        in_specs=[anywhere] * 12,
        out_specs=(vmem, vmem, vmem),
        scratch_shapes=[
            pltpu.VMEM(sign_bits.shape, jnp.int32),
            pltpu.VMEM(positions.shape, jnp.int32),
            pltpu.VMEM((2 * N, 2 * N), bf16),
            pltpu.VMEM((2 * N, 2 * N), bf16),
            pltpu.VMEM((2 * N, N), bf16),
            pltpu.VMEM((2 * N, N), bf16),
            pltpu.VMEM((2 * N, N), bf16),
            pltpu.VMEM((2 * N, N), bf16),
            pltpu.VMEM((2 * N, 2 * N), bf16),
            pltpu.VMEM((2 * N, 2 * N), bf16),
            pltpu.VMEM((slots, CHIPS * MSG, LANES), f32),
            pltpu.VMEM((slots, CHIPS * MSG, LANES), f32),
            pltpu.VMEM((ROWS, 2 * N), f32),
            pltpu.VMEM((ROWS, 2 * N), f32),
            pltpu.VMEM((4, N, 2 * N), f32),
            pltpu.VMEM((2 * N, 2 * N), f32),
            pltpu.VMEM((ROWS, 2 * N), bf16),
            pltpu.VMEM((ROWS, 2 * N), bf16),
            pltpu.VMEM((ROWS, N), f32),
            pltpu.VMEM((ROWS, N), f32),
            pltpu.VMEM((2, ROWS, N), f32),
            pltpu.SemaphoreType.DMA((slots,)),
            pltpu.SemaphoreType.DMA((slots,)),
            pltpu.SemaphoreType.DMA((12,)),
            pltpu.SemaphoreType.DMA((ROWS // N,)),
            pltpu.SemaphoreType.DMA((ROWS // N,)),
        ],
        compiler_params=pltpu.CompilerParams(
            collective_id=0, has_side_effects=True, vmem_limit_bytes=44 << 20
        ),
    )(
        in_hbm(speed.reshape(ROWS, N)),
        in_hbm(sign_bits),
        in_hbm(positions),
        in_hbm(observed.reshape(2, ROWS, N)),
        *[in_hbm(jnp.asarray(t)) for t in tables()],
    )
    field, gradient = pl.pallas_call(
        close,
        out_shape=(
            pltpu.HBM((2, ROWS, N), f32),
            pltpu.HBM((ROWS, LANES), f32),
        ),
        in_specs=[anywhere, vmem, vmem],
        out_specs=(anywhere, anywhere),
        scratch_shapes=[
            pltpu.VMEM((ROWS, LANES), f32),
            pltpu.SemaphoreType.DMA((2,)),
        ],
        compiler_params=pltpu.CompilerParams(vmem_limit_bytes=4 << 20),
    )(*[pltpu.with_memory_space_constraint(a, pltpu.VMEM) for a in (field, term, other)])
    return field.reshape(1, 2, BLOCK, BLOCK, N), gradient.reshape(BLOCK, BLOCK, LANES)


def solution(mesh):
    return jax.shard_map(
        per_device,
        mesh=mesh,
        in_specs=(P("pz", "py", None), P("src", None), P(), P("src", None, "pz", "py", None)),
        out_specs=(P("src", None, "pz", "py", None), P("pz", "py", "src")),
        check_vma=False,
    )
```

```python
import functools
import math

import jax
import jax.numpy as jnp
import numpy as np
from jax import lax
from jax.experimental import pallas as pl
from jax.experimental.pallas import tpu as pltpu
from jax.sharding import PartitionSpec as P

MESH = pl.DeviceIdType.MESH
N = 256
SIDE = 8
CHIPS = SIDE * SIDE
BLOCK = N // SIDE
ROWS = BLOCK * BLOCK
LANES = 128
HALVES = 2
PIECES = 4
TILES = 4 // PIECES
MSG = TILES * 8
ORDER = [
    42, 58, 41, 46, 38, 43, 26, 47, 59, 54, 25, 62, 57, 22, 34, 30, 40, 27, 37, 39, 45,
    10, 31, 53, 61, 23, 6, 44, 11, 33, 29, 55, 50, 24, 14, 36, 21, 63, 35, 9, 56, 18,
    51, 13, 20, 60, 17, 7, 49, 8, 19, 28, 2, 52, 5, 32, 15, 3, 16, 48, 4, 1, 12,
]

wave_sq = (2.0 * math.pi / 8.0) ** 2
damping = 0.05
source_gain = 40.0


def tables():
    angle = lambda a, b: 2.0 * np.pi * ((a[:, None] * b[None, :]) % N) / N
    count = np.arange(N)
    chip = np.arange(CHIPS)
    freq = np.stack([2 * chip + 1, N - 1 - 2 * chip, 2 * chip, (N - 2 * chip) % N], 1)
    freq[0, 3] = N // 2
    rows = []
    for half in range(HALVES):
        for member in range(2):
            turn = angle(freq[:, 2 * half + member], count)
            rows.append(np.concatenate([np.cos(turn), np.sin(turn)], 1))
            rows.append(np.concatenate([-np.sin(turn), np.cos(turn)], 1))
    along_x = np.concatenate(rows, 0)
    turn = angle(count, count)
    cosine, sine = np.cos(turn), np.sin(turn)
    along_y = np.block([[cosine, -sine], [sine, cosine]])
    order = z_of_row(count)
    forward = np.concatenate([cosine[:, order], sine[:, order]], 0)
    backward = np.concatenate([cosine[order], sine[order]], 0)
    out = []
    for table in (along_y, forward, backward, along_x):
        high = table.astype(jnp.bfloat16)
        out += [high, (table - high.astype(np.float64)).astype(jnp.bfloat16)]
    return out


def z_of_row(row):
    per = N // PIECES
    piece, rest = row // per, row % per
    s, rest = rest // (16 * TILES), rest % (16 * TILES)
    j, rest = rest // (2 * TILES), rest % (2 * TILES)
    return j * BLOCK + 8 * (piece * TILES) + 4 * rest + s


def split(value):
    high = value.astype(jnp.bfloat16)
    return high, (value - high.astype(jnp.float32)).astype(jnp.bfloat16)


def times(value, high, low):
    first, rest = split(value)
    dot = functools.partial(jnp.dot, preferred_element_type=jnp.float32)
    return dot(first, high) + (dot(first, low) + dot(rest, high))


def times_left(high, low, value):
    first, rest = split(value)
    dot = functools.partial(jnp.dot, preferred_element_type=jnp.float32)
    return dot(high, first) + (dot(low, first) + dot(high, rest))


def swap(parts):
    lane = lax.broadcasted_iota(jnp.int32, parts[0].shape, 1)
    odd, upper = (lane & 32) != 0, (lane & 64) != 0
    mid = []
    for b in (0, 2):
        low, high = parts[b], parts[b + 1]
        mid.append(jnp.where(odd, pltpu.roll(high, 32, 1), low))
        mid.append(jnp.where(odd, high, pltpu.roll(low, 96, 1)))
    out = [None] * 4
    for b in (0, 1):
        low, high = mid[b], mid[b + 2]
        out[b] = jnp.where(upper, pltpu.roll(high, 64, 1), low)
        out[b + 2] = jnp.where(upper, high, pltpu.roll(low, 64, 1))
    return out


def kernel(
    speed_hbm, bits_hbm, pos_hbm, seen_hbm, yh_hbm, yl_hbm, fh_hbm, fl_hbm, bh_hbm, bl_hbm, xh_hbm, xl_hbm,
    field, term, other,
    bits_ref, pos_ref, yh, yl, fh, fl, bh, bl, xh, xl, sent, got, acc, first, green, plane, drive_h, drive_l, source, speed, seen,
    send_sem, recv_sem, load_sem, pair_send, pair_recv,
):
    core, py, pz = lax.axis_index("src"), lax.axis_index("py"), lax.axis_index("pz")
    me = py * SIDE + pz
    X, ZH, Y, ZL = py >> 1, py & 1, pz >> 1, pz & 1
    Z = 2 * ZH + ZL

    def partner(o):
        x, y, z = (X + (o >> 4)) & 3, (Y + ((o >> 2) & 3)) & 3, (Z + (o & 3)) & 3
        return 2 * x + (z >> 1), 2 * y + (z & 1)

    pairs = ((bits_hbm, bits_ref), (pos_hbm, pos_ref), (yh_hbm, yh), (yl_hbm, yl), (fh_hbm, fh), (fl_hbm, fl), (bh_hbm, bh), (bl_hbm, bl),
             (xh_hbm, xh), (xl_hbm, xl), (speed_hbm, speed), (seen_hbm, seen))
    loads = [pltpu.make_async_copy(a, b, load_sem.at[n]) for n, (a, b) in enumerate(pairs)]
    for load in loads[:2]:
        load.start()
    barrier = pltpu.get_barrier_semaphore()

    for o in ORDER:
        a, b = partner(o)
        pl.semaphore_signal(barrier, inc=1, device_id={"py": a, "pz": b}, device_id_type=MESH)

    pl.semaphore_signal(barrier, inc=1, device_id={"src": 1 - core}, device_id_type=MESH)

    for load in loads[2:]:
        load.start()

    def slot(phase, half, piece):
        return (phase * HALVES + half) * PIECES + piece

    def send(phase, half, piece):
        n = slot(phase, half, piece)
        mine = pl.ds(pl.multiple_of(me * MSG, MSG), MSG)

        for o in ORDER:
            a, b = partner(o)
            theirs = pl.ds(pl.multiple_of((a * SIDE + b) * MSG, MSG), MSG)
            pltpu.make_async_remote_copy(
                src_ref=sent.at[n, theirs],
                dst_ref=got.at[n, mine],
                send_sem=send_sem.at[n],
                recv_sem=recv_sem.at[n],
                device_id={"py": a, "pz": b},
                device_id_type=MESH,
            ).start()

        got[n, mine] = sent[n, mine]

    def finish(n, sem):
        everyone = got.at[n, pl.ds(0, (CHIPS - 1) * MSG)]
        pltpu.make_async_copy(everyone, everyone, sem.at[n]).wait()

    def arrive(phase, half, piece):
        finish(slot(phase, half, piece), recv_sem)

    def wave_of(index):
        signed = jnp.where(index < N // 2, index, index - N)
        return signed.astype(jnp.float32) * (2.0 * math.pi / N)

    row_id = lax.broadcasted_iota(jnp.int32, (N, N), 0)
    lane_id = lax.broadcasted_iota(jnp.int32, (N, N), 1)
    base = wave_of(row_id) ** 2 + wave_of(lane_id) ** 2

    def green_of(half, member):
        index = 2 * me + 1 - half
        if half == 1 and member == 1:
            index = jnp.where(me == 0, N // 2, index)
        wave = index.astype(jnp.float32) * (2.0 * math.pi / N)
        shifted = base + wave * wave - wave_sq
        scale = (1.0 / N**3) / (shifted * shifted + damping * damping)
        green[2 * half + member, :, 0:N] = shifted * scale
        green[2 * half + member, :, N : 2 * N] = damping * scale

    def spectrum_z(value):
        both = times_left(fh[...], fl[...], value)
        real = both[:N, :N] + both[N:, N:]
        imag = both[:N, N:] - both[N:, :N]
        return real, imag

    def filtered(half, member, real, imag):
        g_re = green[2 * half + member, :, 0:N]
        g_im = green[2 * half + member, :, N : 2 * N]
        plane[member * N : (member + 1) * N, 0:N] = real * g_im + imag * g_re
        plane[member * N : (member + 1) * N, N : 2 * N] = real * g_re - imag * g_im

    def inverse_pieces(phase, half, pieces, conjugate):
        size = 16 * TILES
        high = 4 * size
        if len(pieces) == PIECES:
            table_h, table_l = bh[...], bl[...]
        else:
            at = pieces[0] * high
            table_h = jnp.concatenate([bh[at : at + high, :], bh[N + at : N + at + high, :]], 0)
            table_l = jnp.concatenate([bl[at : at + high, :], bl[N + at : N + at + high, :]], 0)
        high = high * len(pieces)
        for member in range(2):
            both = times_left(table_h, table_l, plane[member * N : (member + 1) * N, :])
            real = both[:high, N:] - both[high:, :N]
            imag = both[:high, :N] + both[high:, N:]
            if conjugate and member == 0:
                imag = -imag
            for part, value in ((0, real), (1, imag)):
                for place, piece in enumerate(pieces):
                    n = slot(phase, half, piece)
                    for h in range(2):
                        rows = [
                            value[(place * 4 + s) * size : (place * 4 + s + 1) * size, h * LANES : (h + 1) * LANES]
                            for s in range(4)
                        ]
                        for b, block in enumerate(swap(rows)):
                            start = (4 * h + b) * SIDE * MSG + 2 * member + part
                            sent[n, pl.ds(start, size, stride=4), :] = block

    def inverse(phase, half):
        plane[...] = times(plane[...], yh[...], yl[...])
        inverse_pieces(phase, half, range(PIECES), False)

    def gather(phase, half):
        size = 16 * TILES
        for piece in range(PIECES):
            n = slot(phase, half, piece)
            for member in range(2):
                for part in range(2):
                    for h in range(2):
                        rows = [
                            got[n, pl.ds((4 * h + b) * SIDE * MSG + 2 * member + part, size, stride=4), :]
                            for b in range(4)
                        ]
                        for s, block in enumerate(swap(rows)):
                            at = member * N + (piece * 4 + s) * size
                            plane[at : at + size, part * N + h * LANES : part * N + (h + 1) * LANES] = block

    for load in loads[:2]:
        load.wait()
    weight = (2 * bits_ref[...] - 1).astype(jnp.float32) * source_gain
    emitters = weight.shape[1]
    z_at, y_at, x_at = pos_ref[0:1, :], pos_ref[1:2, :], pos_ref[2:3, :]
    ids = lax.broadcasted_iota(jnp.int32, (N, emitters), 0)

    def hits(where, index):
        return jnp.where(where == index, 1.0, 0.0).astype(jnp.bfloat16)

    which = lax.broadcasted_iota(jnp.int32, (8, N), 0)
    turn = lax.broadcasted_iota(jnp.int32, (8, N), 1)
    only = jnp.logical_and(which == 3, me == 0)
    turn = (turn * jnp.where(only, N // 2, 2 * me + jnp.where(which < 2, 1, 0))) & (N - 1)
    shift = jnp.where(jnp.logical_and(which % 2 == 1, jnp.logical_not(only)), math.pi / 2.0, 0.0)
    wave_rows = jnp.cos(turn.astype(jnp.float32) * (2.0 * math.pi / N) - shift)
    wh, wl = split(wave_rows)
    x_hits = hits(x_at, ids)
    phases = jnp.dot(wh, x_hits, preferred_element_type=jnp.float32) + jnp.dot(
        wl, x_hits, preferred_element_type=jnp.float32
    )
    phases = phases * weight
    y_hits = hits(y_at, ids)
    z_equal = z_at == z_of_row(ids)

    nt = (((1,), (1,)), ((), ()))
    for half in range(HALVES):
        for member in range(2):
            row = phases[2 * half + member : 2 * half + member + 1, :]
            high = row.astype(jnp.bfloat16).astype(jnp.float32)
            value = 0.0
            for piece_row in (high, row - high):
                left = jnp.where(z_equal, piece_row, 0.0).astype(jnp.bfloat16)
                value = value + lax.dot_general(left, y_hits, nt, preferred_element_type=jnp.float32)
            if half == 0:
                plane[0:N, member * N : (member + 1) * N] = value
            else:
                plane[member * N : (member + 1) * N, 0:N] = value
        for member in range(2):
            green_of(half, member)
        if half == 0:
            for load in loads[2:8]:
                load.wait()
            real, imag = spectrum_z(times(plane[0:N, :], yh[...], yl[...]))
            g_re, g_im = green[0, :, 0:N], green[0, :, N : 2 * N]
            rr, ii, ri, ir = real * g_re, imag * g_im, real * g_im, imag * g_re
            plane[0:N, 0:N], plane[0:N, N : 2 * N] = ir - ri, rr + ii
            plane[N : 2 * N, 0:N], plane[N : 2 * N, N : 2 * N] = ir + ri, rr - ii
            plane[...] = times(plane[...], yh[...], yl[...])
            for piece in range(PIECES):
                inverse_pieces(0, 0, [piece], True)
                if piece == 0:
                    pl.semaphore_wait(barrier, CHIPS)
                send(0, 0, piece)
        else:
            lines = times(plane[:, 0:N], yh[0:N, :], yl[0:N, :])
            one_re, one_im = spectrum_z(lines[:N])
            two_re, two_im = spectrum_z(lines[N:])
            alone = me == 0
            filtered(1, 0, jnp.where(alone, one_re, one_re + two_im), jnp.where(alone, one_im, one_im - two_re))
            filtered(1, 1, jnp.where(alone, two_re, one_re - two_im), jnp.where(alone, two_im, one_im + two_re))
            inverse(0, 1)
            for piece in range(PIECES):
                send(0, 1, piece)

    local_z, local_y = z_at - pz * BLOCK, y_at - py * BLOCK
    inside = (local_z >= 0) & (local_z < BLOCK) & (local_y >= 0) & (local_y < BLOCK)
    cell = jnp.where(inside, local_z * BLOCK + local_y, -1)
    lines = jnp.where(x_at == ids, weight, 0.0).astype(jnp.bfloat16)

    @pl.loop(0, ROWS // N)
    def _(g):
        at = pl.multiple_of(g * N, N)
        source[pl.ds(at, N), :] = lax.dot_general(
            hits(cell - at, ids), lines, nt, preferred_element_type=jnp.float32
        )

    for load in loads[8:11]:
        load.wait()

    def x_inverse(phase, half, piece, tile, r):
        n = slot(phase, half, piece)
        rows = [got[n, pl.ds(tile * 8 + r * 4 + kc, CHIPS, stride=MSG), :] for kc in range(4)]
        return times(jnp.concatenate(rows, 0).T, xh[half * N : (half + 1) * N, :], xl[half * N : (half + 1) * N, :])

    def x_forward(phase, half, piece, tile):
        n = slot(phase, half, piece)
        at = pl.multiple_of((piece * TILES + tile) * N, N)
        high, low = drive_h[pl.ds(at, N), :], drive_l[pl.ds(at, N), :]
        table_h, table_l = xh[half * N : (half + 1) * N, :], xl[half * N : (half + 1) * N, :]
        dot = lambda a, b: lax.dot_general(a, b, nt, preferred_element_type=jnp.float32)
        out = dot(table_h, high) + (dot(table_l, high) + dot(table_h, low))
        for r in range(2):
            for kc in range(4):
                sent[n, pl.ds(tile * 8 + r * 4 + kc, CHIPS, stride=MSG), :] = out[
                    kc * CHIPS : (kc + 1) * CHIPS, r * LANES : (r + 1) * LANES
                ]

    def half_inverse(phase):
        for piece in range(PIECES):
            arrive(phase, 0, piece)

            @pl.loop(0, TILES)
            def _(tile):
                for r in range(2):
                    at = pl.multiple_of((piece * TILES + tile) * N + r * LANES, LANES)
                    acc[pl.ds(at, LANES), :] = x_inverse(phase, 0, piece, tile, r)

    def medium(at):
        v = speed[pl.ds(at, LANES), :]
        inverse_sq = 1.0 / (v * v)
        real_v = wave_sq * (inverse_sq - 1.0)
        return v, inverse_sq, real_v

    half_inverse(0)
    for piece in range(PIECES):
        arrive(0, 1, piece)

        @pl.loop(0, TILES)
        def _(tile):
            for r in range(2):
                at = pl.multiple_of((piece * TILES + tile) * N + r * LANES, LANES)
                here = pl.ds(at, LANES)
                spread = acc[here, :] + x_inverse(0, 1, piece, tile, r)
                spread_re, spread_im = spread[:, :N], spread[:, N:]
                _, _, real_v = medium(at)
                ratio = real_v / damping
                real, imag = spread_re - ratio * spread_im, spread_im + ratio * spread_re
                first[here, 0:N] = real
                first[here, N : 2 * N] = imag
                drive_re = real_v * real + damping * imag + source[here, :]
                drive_im = real_v * imag - damping * real
                for part, value in ((0, drive_re), (1, drive_im)):
                    high, low = split(value)
                    drive_h[here, part * N : (part + 1) * N] = high
                    drive_l[here, part * N : (part + 1) * N] = low
            x_forward(1, 0, piece, tile)

        send(1, 0, piece)
    for piece in range(PIECES):

        @pl.loop(0, TILES)
        def _(tile):
            x_forward(1, 1, piece, tile)

        send(1, 1, piece)

    for half in range(HALVES):
        for piece in range(PIECES):
            arrive(1, half, piece)
        gather(1, half)
        plane[...] = times(plane[...], yh[...], yl[...])
        for member in range(2):
            real, imag = spectrum_z(plane[member * N : (member + 1) * N, :])
            filtered(half, member, real, imag)
        inverse(2, half)
        for piece in range(PIECES):
            send(2, half, piece)

    half_inverse(2)
    loads[11].wait()

    def tell(n):
        rows = pl.ds(pl.multiple_of(n * N, N), N)
        return pltpu.make_async_remote_copy(
            src_ref=term.at[1, rows],
            dst_ref=other.at[rows],
            send_sem=pair_send.at[n],
            recv_sem=pair_recv.at[n],
            device_id={"src": 1 - core},
            device_id_type=MESH,
        )

    for piece in range(PIECES):
        arrive(2, 1, piece)

        @pl.loop(0, TILES)
        def _(tile):
            for r in range(2):
                at = pl.multiple_of((piece * TILES + tile) * N + r * LANES, LANES)
                here = pl.ds(at, LANES)
                spread = acc[here, :] + x_inverse(2, 1, piece, tile, r)
                was_re, was_im = first[here, 0:N], first[here, N : 2 * N]
                delta_re, delta_im = spread[:, :N] - was_re, spread[:, N:] - was_im
                v, inverse_sq, real_v = medium(at)
                ratio = real_v / damping
                real = was_re + delta_re - ratio * delta_im
                imag = was_im + delta_im + ratio * delta_re
                field[0, here, :] = real
                field[1, here, :] = imag
                misfit = (real - seen[0, here, :]) * real + (imag - seen[1, here, :]) * imag
                part = misfit * (-2.0 * wave_sq) * inverse_sq / v
                term[0, here, :] = jnp.where(core == 0, part[:, :LANES], part[:, LANES:])
                term[1, here, :] = jnp.where(core == 0, part[:, LANES:], part[:, :LANES])

            tell(piece * TILES + tile).start()

    for n in range(3 * HALVES * PIECES):
        finish(n, send_sem)
    for n in range(ROWS // N):
        tell(n).wait()


def close(field, term, other, field_out, gradient_out, total, sem):
    put_field = pltpu.make_async_copy(field, field_out, sem.at[0])
    put_field.start()
    total[...] = term[0] + other[...]
    put_total = pltpu.make_async_copy(total, gradient_out, sem.at[1])
    put_total.start()
    put_field.wait()
    put_total.wait()


def per_device(speed, sign_bits, positions, observed):
    f32, bf16 = jnp.float32, jnp.bfloat16
    anywhere = pl.BlockSpec(memory_space=pl.ANY)
    vmem = pl.BlockSpec(memory_space=pltpu.VMEM)
    slots = 3 * HALVES * PIECES
    in_hbm = lambda a: pltpu.with_memory_space_constraint(a, pltpu.HBM)
    field, term, other = pl.pallas_call(
        kernel,
        out_shape=(
            pltpu.VMEM((2, ROWS, N), f32),
            pltpu.VMEM((2, ROWS, LANES), f32),
            pltpu.VMEM((ROWS, LANES), f32),
        ),
        in_specs=[anywhere] * 12,
        out_specs=(vmem, vmem, vmem),
        scratch_shapes=[
            pltpu.VMEM(sign_bits.shape, jnp.int32),
            pltpu.VMEM(positions.shape, jnp.int32),
            pltpu.VMEM((2 * N, 2 * N), bf16),
            pltpu.VMEM((2 * N, 2 * N), bf16),
            pltpu.VMEM((2 * N, N), bf16),
            pltpu.VMEM((2 * N, N), bf16),
            pltpu.VMEM((2 * N, N), bf16),
            pltpu.VMEM((2 * N, N), bf16),
            pltpu.VMEM((2 * N, 2 * N), bf16),
            pltpu.VMEM((2 * N, 2 * N), bf16),
            pltpu.VMEM((slots, CHIPS * MSG, LANES), f32),
            pltpu.VMEM((slots, CHIPS * MSG, LANES), f32),
            pltpu.VMEM((ROWS, 2 * N), f32),
            pltpu.VMEM((ROWS, 2 * N), f32),
            pltpu.VMEM((4, N, 2 * N), f32),
            pltpu.VMEM((2 * N, 2 * N), f32),
            pltpu.VMEM((ROWS, 2 * N), bf16),
            pltpu.VMEM((ROWS, 2 * N), bf16),
            pltpu.VMEM((ROWS, N), f32),
            pltpu.VMEM((ROWS, N), f32),
            pltpu.VMEM((2, ROWS, N), f32),
            pltpu.SemaphoreType.DMA((slots,)),
            pltpu.SemaphoreType.DMA((slots,)),
            pltpu.SemaphoreType.DMA((12,)),
            pltpu.SemaphoreType.DMA((ROWS // N,)),
            pltpu.SemaphoreType.DMA((ROWS // N,)),
        ],
        compiler_params=pltpu.CompilerParams(
            collective_id=0, has_side_effects=True, vmem_limit_bytes=44 << 20
        ),
    )(
        in_hbm(speed.reshape(ROWS, N)),
        in_hbm(sign_bits),
        in_hbm(positions),
        in_hbm(observed.reshape(2, ROWS, N)),
        *[in_hbm(jnp.asarray(t)) for t in tables()],
    )
    field, gradient = pl.pallas_call(
        close,
        out_shape=(
            pltpu.HBM((2, ROWS, N), f32),
            pltpu.HBM((ROWS, LANES), f32),
        ),
        in_specs=[anywhere, vmem, vmem],
        out_specs=(anywhere, anywhere),
        scratch_shapes=[
            pltpu.VMEM((ROWS, LANES), f32),
            pltpu.SemaphoreType.DMA((2,)),
        ],
        compiler_params=pltpu.CompilerParams(vmem_limit_bytes=4 << 20),
    )(*[pltpu.with_memory_space_constraint(a, pltpu.VMEM) for a in (field, term, other)])
    return field.reshape(1, 2, BLOCK, BLOCK, N), gradient.reshape(BLOCK, BLOCK, LANES)


def solution(mesh):
    return jax.shard_map(
        per_device,
        mesh=mesh,
        in_specs=(P("pz", "py", None), P("src", None), P(), P("src", None, "pz", "py", None)),
        out_specs=(P("src", None, "pz", "py", None), P("pz", "py", "src")),
        check_vma=False,
    )
```
